32 devices in a mesh: dp: 8 (over y, x, core), ctx: 4 (over z).
Axes of the slice: x: 2, y: 2, z: 4, core: 2. Of those that a mesh axis runs over, the one named last changes fastest.
Arguments:
- tokens: bfloat16 [12288, 1536], P(('dp', 'ctx')), may hold values from -6 to 6
- seq_lens: int32 [8], P('dp'), may hold values from 1153 to 1536, as said below
- gain_in: bfloat16 [1536], P(('dp', 'ctx')), may hold values from 0.099609375 to 1.8984375
- w_query: bfloat16 [1536, 1536], P(('dp', 'ctx')), may hold values from -0.15625 to 0.15625
- w_key: bfloat16 [1536, 512], P(('dp', 'ctx')), may hold values from -0.15625 to 0.15625
- w_value: bfloat16 [1536, 512], P(('dp', 'ctx')), may hold values from -0.15625 to 0.15625
- w_out: bfloat16 [1536, 1536], P(None, ('dp', 'ctx')), may hold values from -3.5 to 3.5
- qk_gains: bfloat16 [128], P(('dp', 'ctx')), may hold values from 0.099609375 to 1.8984375
- gain_mid: bfloat16 [1536], P(('dp', 'ctx')), may hold values from 0.099609375 to 1.8984375
- w_gate: bfloat16 [1536, 6912], P('dp', 'ctx'), may hold values from -0.15625 to 0.15625
- w_up: bfloat16 [1536, 6912], P('dp', 'ctx'), may hold values from -0.15625 to 0.15625
- w_down: bfloat16 [6912, 1536], P('ctx', 'dp'), may hold values from -0.078125 to 0.078125
- grad_out: bfloat16 [12288, 1536], P(('dp', 'ctx')), may hold values from -6 to 6
Outputs:
- output: bfloat16 [12288, 1536], P(('dp', 'ctx'))
- grad_tokens: float32 [12288, 1536], P(('dp', 'ctx'))
- grad_gain_in: float32 [1536], P(('dp', 'ctx'))
- grad_w_query: float32 [1536, 1536], P(('dp', 'ctx'))
- grad_w_key: float32 [1536, 512], P(('dp', 'ctx'))
- grad_w_value: float32 [1536, 512], P(('dp', 'ctx'))
- grad_w_out: float32 [1536, 1536], P(None, ('dp', 'ctx'))
- grad_qk_gains: float32 [128], P(('dp', 'ctx'))
- grad_gain_mid: float32 [1536], P(('dp', 'ctx'))
- grad_w_gate: float32 [1536, 6912], P('dp', 'ctx')
- grad_w_up: float32 [1536, 6912], P('dp', 'ctx')
- grad_w_down: float32 [6912, 1536], P('ctx', 'dp')
The draws below stay inside these ranges and needn't reach their ends.
Inputs may be any that keep to these rules, and one draw needn't show every extreme that they name: `seq_lens`: one valid length per sequence slot; in every draw some sequence has exactly 1536.
All inputs are finite; a program needn't handle non-finite values.
Results may differ from the reference program's by a relative error of at most 0.018.
Values may be sent and summed in bfloat16 or wider, within the bound.
A program may use at most 448 MiB of HBM per device.

```python
import jax
import jax.numpy as jnp
from jax import lax

D = 1536
H = 24
KVH = 8
HD = 64
FF = 6912
SEQ = 1536
SEQS = 8
TOKENS = 12288


def draw_seq_lens(key, part):
    first_key, second_key = jax.random.split(jax.random.fold_in(key, 17))
    lengths = jax.random.randint(first_key, (SEQS,), 3 * SEQ // 4 + 1, SEQ + 1)
    longest = jax.random.randint(second_key, (), 0, SEQS)
    return jnp.where(jnp.arange(SEQS) == longest, SEQ, lengths).astype(jnp.int32)


def raised(values, stream_key, source, target, blocks, factor):
    def block_of(axis_at):
        return (jnp.arange(values.shape[axis_at]) // (values.shape[axis_at] // blocks)).reshape((-1,) + (1,) * (values.ndim - 1 - axis_at))

    first = jax.random.permutation(stream_key, blocks)[block_of(target)]
    other_side = (block_of(target) + blocks // 2) % blocks
    return jnp.where((block_of(source) == first) | (block_of(source) == other_side), factor * values, values)


def block_levels(rng, dims, shards, smallest, high):
    level = 1.0
    for dim, shards_of in shards:
        draws = jax.random.uniform(jax.random.fold_in(jax.random.fold_in(rng, 6), dim), (shards_of,), jnp.float32, smallest / len(shards), high / len(shards))
        level = level * jnp.repeat(jnp.exp(draws), dims[dim] // shards_of).reshape((-1,) + (1,) * (len(dims) - 1 - dim))
    return level


def centred(rng, dims, width, bound, cuts=(), held_as=jnp.bfloat16):
    loudness = block_levels(rng, dims, cuts, -0.22, 0.18) if cuts else 1.0
    result = jax.random.normal(rng, dims, jnp.float32) * width * loudness
    return jnp.minimum(jnp.maximum(result, -bound), bound).astype(held_as)


def bell_draw_with(rng, dims, scale, reach, cuts, heavy, kind=jnp.bfloat16):
    drawn = scale * jax.random.normal(rng, dims, jnp.float32)
    if cuts:
        drawn = drawn * block_levels(rng, dims, cuts, -0.22, 0.18)
    return jnp.clip(raised(drawn, jax.random.fold_in(rng, 3), *heavy), -reach, reach).astype(kind)


def setup_inputs(seed: int = 0) -> dict:
    splits = jax.random.split(jax.random.key(seed), 14)
    return {
        "tokens": bell_draw_with(splits[0], (TOKENS, D), 1.0, 6.0, ((0, 32),), (0, 1, 32, 2.75)),
        "seq_lens": draw_seq_lens(jax.random.fold_in(splits[13], 71), 0),
        "gain_in": jnp.clip(1.0 + 0.18 * jax.random.normal(splits[2], (D,), jnp.float32), 0.099609375, 1.8984375).astype(jnp.bfloat16),
        "w_query": centred(splits[3], (D, H * HD), D ** -0.5, 0.15625, ((0, 32),)),
        "w_key": centred(splits[4], (D, KVH * HD), D ** -0.5, 0.15625, ((0, 32),)),
        "w_value": centred(splits[5], (D, KVH * HD), D ** -0.5, 0.15625, ((0, 32),)),
        "w_out": centred(splits[6], (H * HD, D), (max(H * HD // 512, 1)) ** -0.5, 3.5, ((1, 32),)),
        "qk_gains": jnp.clip(1.0 + 0.18 * jax.random.normal(splits[7], (2 * HD,), jnp.float32), 0.099609375, 1.8984375).astype(jnp.bfloat16),
        "gain_mid": jnp.clip(1.0 + 0.18 * jax.random.normal(splits[8], (D,), jnp.float32), 0.099609375, 1.8984375).astype(jnp.bfloat16),
        "w_gate": centred(splits[9], (D, FF), D ** -0.5, 0.15625, ((0, 8), (1, 4))),
        "w_up": centred(splits[10], (D, FF), D ** -0.5, 0.15625, ((0, 8), (1, 4))),
        "w_down": centred(splits[11], (FF, D), FF ** -0.5, 0.078125, ((0, 4), (1, 8))),
        "grad_out": bell_draw_with(splits[12], (TOKENS, D), 1.0, 6.0, ((0, 32),), (0, 1, 32, 2.75)),
    }


EPSILON = 1e-05
THETA = 1000000.0
NEG_BIG = -1e+30

@jax.custom_vjp
def low(v):
    return lax.optimization_barrier(v.astype(jnp.bfloat16)).astype(jnp.float32)

@jax.custom_vjp
def low_back(v):
    return v

def low_keep(v):
    return (low(v), None)

def low_pass(kept, grad):
    return (grad,)

def back_keep(v):
    return (v, None)

def back_low(kept, grad):
    return (low(grad),)
low.defvjp(low_keep, low_pass)
low_back.defvjp(back_keep, back_low)

def matmul(left, right):
    return jnp.dot(left, right, precision=lax.Precision.HIGHEST, preferred_element_type=jnp.float32)

def rms_scale(values, gain_vec):
    return values * lax.rsqrt(lax.optimization_barrier(jnp.mean(values * values, axis=-1, keepdims=True)) + EPSILON) * gain_vec

def rotate(values, positions):
    half_width = values.shape[-1] // 2
    frequency = THETA ** (-jnp.arange(half_width, dtype=jnp.float32) * 2.0 / values.shape[-1])
    angles = positions.astype(jnp.float32)[:, None] * frequency[None, :]
    cosine_table = jnp.concatenate([jnp.cos(angles), jnp.cos(angles)], -1)[:, None, :]
    sine_table = jnp.concatenate([jnp.sin(angles), jnp.sin(angles)], -1)[:, None, :]
    turned = jnp.concatenate([-values[..., half_width:], values[..., :half_width]], -1)
    return values * cosine_table + turned * sine_table

def sequence_layer(seq_rows, length, gain_in, w_query, w_key, w_value, w_out, qk_gains, gain_mid, w_gate, w_up, w_down):
    positions = jnp.arange(SEQ, dtype=jnp.int32)
    group_size = H // KVH
    normed = low(rms_scale(seq_rows, gain_in))
    query_rows = low_back(matmul(normed, w_query)).reshape(SEQ, H, HD)
    key_rows = low_back(matmul(normed, w_key)).reshape(SEQ, KVH, HD)
    value_rows = low(low_back(matmul(normed, w_value))).reshape(SEQ, KVH, HD)
    query_rows = low(rotate(rms_scale(query_rows, qk_gains[:HD]), positions))
    key_rows = low(rotate(rms_scale(key_rows, qk_gains[HD:]), positions))
    allowed = (positions[None, :] <= positions[:, None]) & (positions[None, :] < length)

    def one_head(pieces):
        query_part, key_part, value_part = pieces
        scores = jnp.einsum('tgd,jd->tgj', query_part, key_part, precision=lax.Precision.HIGHEST) * HD ** (-0.5)
        scores = low_back(scores)
        scores = jnp.where(allowed[:, None, :], scores, NEG_BIG)
        probs_full = jax.nn.softmax(scores, axis=-1)
        return low_back(jnp.einsum('tgj,jd->tgd', low(probs_full), value_part, precision=lax.Precision.HIGHEST))
    grouped = query_rows.reshape(SEQ, KVH, group_size, HD).transpose(1, 0, 2, 3)
    mixed_heads = lax.map(jax.checkpoint(one_head), (grouped, key_rows.transpose(1, 0, 2), value_rows.transpose(1, 0, 2)))
    mixed_rows = low(mixed_heads.transpose(1, 0, 2, 3).reshape(SEQ, H * HD))
    hidden = seq_rows + low_back(matmul(mixed_rows, w_out))
    normed_mid = low(rms_scale(hidden, gain_mid))
    gate_proj = low_back(matmul(normed_mid, w_gate))
    up_proj = low_back(matmul(normed_mid, w_up))
    activated = low(jax.nn.silu(gate_proj) * up_proj)
    return hidden + low_back(matmul(activated, w_down))

def reference(tokens, seq_lens, gain_in, w_query, w_key, w_value, w_out, qk_gains, gain_mid, w_gate, w_up, w_down, grad_out):
    params = tuple((weight.astype(jnp.float32) for weight in (gain_in, w_query, w_key, w_value, w_out, qk_gains, gain_mid, w_gate, w_up, w_down)))
    rows_all = tokens.astype(jnp.float32).reshape(SEQS, SEQ, D)
    grads_all = grad_out.astype(jnp.float32).reshape(SEQS, SEQ, D)

    def per_sequence(totals, sequence):
        seq_rows, seq_grads, length = sequence
        valid_rows = (jnp.arange(SEQ, dtype=jnp.int32) < length).astype(jnp.float32)[:, None]

        def apply_layer(seq_input, *layer_params):
            return sequence_layer(seq_input, length, *layer_params)
        seq_output, pullback = jax.vjp(apply_layer, seq_rows, *params)
        grad_list = pullback(seq_grads * valid_rows)
        totals = tuple((total_now + grad_now for total_now, grad_now in zip(totals, grad_list[1:])))
        return (totals, (seq_output, grad_list[0]))
    zero_grads = tuple((jnp.zeros_like(weight) for weight in params))
    totals, (outputs, grad_rows) = lax.scan(per_sequence, zero_grads, (rows_all, grads_all, seq_lens))
    return (outputs.reshape(TOKENS, D).astype(jnp.bfloat16), grad_rows.reshape(TOKENS, D), totals[0], totals[1], totals[2], totals[3], totals[4], totals[5], totals[6], totals[7], totals[8], totals[9])
```

```python
import functools

import jax
import jax.numpy as jnp
from jax import lax
from jax.experimental import pallas as pl
from jax.experimental.pallas import tpu as pltpu
from jax.sharding import PartitionSpec as P

H = 24
KVH = 8
HD = 64
GROUP = H // KVH
PAIRS = KVH // 2


EPSILON = 1e-05
THETA = 1000000.0
NEG_BIG = -1e30

f32 = jnp.float32
bf16 = jnp.bfloat16

NT = (((1,), (1,)), ((), ()))
NN = (((1,), (0,)), ((), ()))


def rms_scale(values, gain_vec):
    factor = lax.rsqrt(jnp.mean(values * values, axis=-1, keepdims=True) + EPSILON)
    return (values * factor * gain_vec, factor)


def norm_back(grad_upper, values, factor, gain_vec):
    unit_rows = values * factor
    scaled = grad_upper * gain_vec
    grad_lower = factor * (
        scaled - unit_rows * jnp.mean(scaled * unit_rows, axis=-1, keepdims=True)
    )
    return (grad_lower, grad_upper * unit_rows)


def rope_tables(positions, head_width):
    half_width = head_width // 2
    frequency = THETA ** (-jnp.arange(half_width, dtype=jnp.float32) * 2.0 / head_width)
    angles = positions.astype(jnp.float32)[:, None] * frequency[None, :]
    cosine_table = jnp.concatenate([jnp.cos(angles), jnp.cos(angles)], -1)[:, None, :]
    sine_table = jnp.concatenate([jnp.sin(angles), jnp.sin(angles)], -1)[:, None, :]
    return (cosine_table, sine_table)


def rotate(values, cosine_table, sine_table):
    half_width = values.shape[-1] // 2
    turned = jnp.concatenate([-values[..., half_width:], values[..., :half_width]], -1)
    return values * cosine_table + turned * sine_table


def rotate_back(grad_upper, cosine_table, sine_table):
    half_width = grad_upper.shape[-1] // 2
    moved_sine = grad_upper * sine_table
    turned = jnp.concatenate([moved_sine[..., half_width:], -moved_sine[..., :half_width]], -1)
    return grad_upper * cosine_table + turned


def mdot(a, b, dims=NN):
    return lax.dot_general(a, b, dims, preferred_element_type=f32)


def causal_mask(rows, limit, key_axis):
    shape = (rows, rows)
    key = lax.broadcasted_iota(jnp.int32, shape, key_axis)
    row = lax.broadcasted_iota(jnp.int32, shape, 1 - key_axis)
    return jnp.where((key <= row) & (key < limit), 0.0, NEG_BIG).astype(f32)


def attn_fwd_kernel(blocks, where_ref, q_ref, *refs):
    kv_refs, (o_ref, log_ref, mask, acc) = refs[:blocks], refs[blocks:]
    rows = q_ref.shape[0]
    mine, limit = where_ref[0], where_ref[1]

    @pl.when(pl.program_id(0) == 0)
    def _():
        mask[...] = causal_mask(rows, limit, 1)

    def head(kv_ref, pair, diagonal):
        keys = kv_ref[0][:, pair * HD : (pair + 1) * HD]
        values = kv_ref[1][:, pair * HD : (pair + 1) * HD]
        extended = jnp.concatenate([values, jnp.ones_like(values)], -1)
        for g in range(GROUP):
            h = pair * GROUP + g
            scores = mdot(q_ref[:, h * HD : (h + 1) * HD], keys, NT)
            if diagonal:
                scores = scores + mask[...]
            term = mdot(jnp.exp(scores).astype(bf16), extended)
            acc[h] = term if diagonal else acc[h] + term

    for pair in range(2):
        head(kv_refs[0], pair, True)
    for back in range(1, blocks):

        @pl.when(mine >= back)
        def _():
            for pair in range(2):
                head(kv_refs[back], pair, False)

    lane = lax.broadcasted_iota(jnp.int32, (rows, 2 * HD), 1)
    logs = jnp.zeros((rows, 2 * HD), f32)
    for h in range(2 * GROUP):
        full = acc[h]
        total = full[:, HD : HD + 1]
        o_ref[:, h * HD : (h + 1) * HD] = (full[:, :HD] / total).astype(bf16)
        logs = jnp.where(lane == h, jnp.log(total), logs)
    log_ref[0] = jnp.transpose(logs)[:8]


def attn_bwd_kernel(blocks, where_ref, q_ref, *refs):
    kv_refs = refs[:blocks]
    do_ref, o_ref, log_ref = refs[blocks : blocks + 3]
    dq_ref = refs[blocks + 3]
    dkv_refs = refs[blocks + 4 : 2 * blocks + 4]
    mask, dqt, inner = refs[2 * blocks + 4 :]
    rows = q_ref.shape[0]
    mine, limit = where_ref[0], where_ref[1]

    @pl.when(pl.program_id(0) == 0)
    def _():
        mask[...] = causal_mask(rows, limit, 0)

    ones = jnp.ones((8, HD), f32)
    for h in range(2 * GROUP):
        cols = slice(h * HD, (h + 1) * HD)
        product = do_ref[:, cols].astype(f32) * o_ref[:, cols].astype(f32)
        inner[h] = lax.dot_general(
            ones, product, NT, preferred_element_type=f32, precision=lax.Precision.HIGHEST
        )

    def head(back, pair):
        cols = slice(pair * HD, (pair + 1) * HD)
        keys = kv_refs[back][0][:, cols]
        values = kv_refs[back][1][:, cols]
        keys_t = jnp.transpose(keys)
        grad_k = jnp.zeros((rows, HD), f32)
        grad_v = jnp.zeros((rows, HD), f32)
        for g in range(GROUP):
            h = pair * GROUP + g
            query = q_ref[:, h * HD : (h + 1) * HD]
            grad = do_ref[:, h * HD : (h + 1) * HD]
            scores = mdot(keys, query, NT) - log_ref[0][h : h + 1]
            if back == 0:
                scores = scores + mask[...]
            probs = jnp.exp(scores)
            gaps = mdot(values, grad, NT) - inner[h][0:1]
            grad_scores = (probs * gaps).astype(bf16)
            grad_k += mdot(grad_scores, query)
            grad_v += mdot(probs.astype(bf16), grad)
            term = mdot(keys_t, grad_scores)
            dqt[h] = term if back == 0 else dqt[h] + term
        dkv_refs[back][0, :, cols] = grad_k.astype(dkv_refs[back].dtype)
        dkv_refs[back][1, :, cols] = grad_v.astype(dkv_refs[back].dtype)

    for pair in range(2):
        head(0, pair)
    for back in range(1, blocks):

        @pl.when(mine >= back)
        def _():
            for pair in range(2):
                head(back, pair)

        @pl.when(mine < back)
        def _():
            dkv_refs[back][...] = jnp.zeros_like(dkv_refs[back])

    for h in range(2 * GROUP):
        dq_ref[:, h * HD : (h + 1) * HD] = jnp.transpose(dqt[h]) * (HD**-0.5)


def kv_spec(rows):
    return pl.BlockSpec((2, rows, 2 * HD), lambda i, *_: (0, 0, i))


def head_spec(rows):
    return pl.BlockSpec((rows, 2 * GROUP * HD), lambda i, *_: (0, i))


def log_spec(rows):
    return pl.BlockSpec((1, 8, rows), lambda i, *_: (i, 0, 0))


def attn_forward(where, query, kv_blocks):
    rows, blocks = query.shape[0], len(kv_blocks)
    return pl.pallas_call(
        functools.partial(attn_fwd_kernel, blocks),
        grid_spec=pltpu.PrefetchScalarGridSpec(
            num_scalar_prefetch=1,
            grid=(PAIRS,),
            in_specs=[head_spec(rows)] + [kv_spec(rows)] * blocks,
            out_specs=[head_spec(rows), log_spec(rows)],
            scratch_shapes=[
                pltpu.VMEM((rows, rows), f32),
                pltpu.VMEM((2 * GROUP, rows, 2 * HD), f32),
            ],
        ),
        out_shape=[
            jax.ShapeDtypeStruct((rows, H * HD), bf16),
            jax.ShapeDtypeStruct((PAIRS, 8, rows), f32),
        ],
        compiler_params=pltpu.CompilerParams(vmem_limit_bytes=48 * 2**20),
        cost_estimate=pl.CostEstimate(
            flops=16 * H * rows * rows * blocks * HD,
            bytes_accessed=8 * rows * H * HD,
            transcendentals=H * rows * rows * blocks,
        ),
        name="attn_forward",
    )(where, query, *kv_blocks)


def attn_backward(where, query, kv_blocks, grad, mixed, logs):
    rows, blocks = query.shape[0], len(kv_blocks)
    kinds = [f32] + [bf16] * (blocks - 1)
    return pl.pallas_call(
        functools.partial(attn_bwd_kernel, blocks),
        grid_spec=pltpu.PrefetchScalarGridSpec(
            num_scalar_prefetch=1,
            grid=(PAIRS,),
            in_specs=[head_spec(rows)]
            + [kv_spec(rows)] * blocks
            + [head_spec(rows), head_spec(rows), log_spec(rows)],
            out_specs=[head_spec(rows)] + [kv_spec(rows)] * blocks,
            scratch_shapes=[
                pltpu.VMEM((rows, rows), f32),
                pltpu.VMEM((2 * GROUP, HD, rows), f32),
                pltpu.VMEM((2 * GROUP, 8, rows), f32),
            ],
        ),
        out_shape=[jax.ShapeDtypeStruct((rows, H * HD), f32)]
        + [jax.ShapeDtypeStruct((2, rows, KVH * HD), kind) for kind in kinds],
        compiler_params=pltpu.CompilerParams(vmem_limit_bytes=56 * 2**20),
        cost_estimate=pl.CostEstimate(
            flops=40 * H * rows * rows * blocks * HD,
            bytes_accessed=20 * rows * H * HD,
            transcendentals=H * rows * rows * blocks,
        ),
        name="attn_backward",
    )(where, query, *kv_blocks, grad, mixed, logs)


def shards(
    tokens,
    seq_lens,
    gain_in,
    w_query,
    w_key,
    w_value,
    w_out,
    qk_gains,
    gain_mid,
    w_gate,
    w_up,
    w_down,
    grad_out,
):
    every = ("dp", "ctx")
    rows, width = tokens.shape
    ctx = lax.axis_size("ctx")
    world = ctx * lax.axis_size("dp")
    mine = lax.axis_index("ctx")
    share = w_query.shape[0]
    qk_share = qk_gains.shape[0]
    positions = mine * rows + jnp.arange(rows, dtype=jnp.int32)
    length = seq_lens[0]
    valid_rows = (positions < length).astype(f32)[:, None]
    where = jnp.stack([mine.astype(jnp.int32), length - mine * rows])
    cosine_table, sine_table = rope_tables(positions, HD)

    def swap(block, r):
        return lax.ppermute(block, "ctx", [(i, i ^ r) for i in range(ctx)])

    def up(block, k):
        return lax.ppermute(block, "ctx", [(i, i + k) for i in range(ctx - k)])

    def down(block, k):
        return lax.ppermute(block, "ctx", [(i + k, i) for i in range(ctx - k)])

    def gather(block, axes):
        return lax.all_gather(block, axes, axis=0, tiled=True)

    def scatter(block, axes):
        return lax.psum_scatter(block, axes, scatter_dimension=0, tiled=True)

    extra = jnp.stack([gain_in, gain_mid, jnp.pad(qk_gains, (0, share - qk_share))], 1)
    extra = jnp.pad(extra, ((0, 0), (0, 125)))
    full_kv = gather(jnp.concatenate([w_key, w_value, extra], 1), every)
    kv_width = 2 * KVH * HD
    full_extra = full_kv[:, kv_width:].astype(f32)
    full_gain_in, full_gain_mid = full_extra[:, 0], full_extra[:, 1]
    full_qk = full_extra[:, 2].reshape(world, share)[:, :qk_share].reshape(-1)
    full_kv = full_kv[:, :kv_width]
    full_query = gather(w_query, every)
    full_out_t = gather(w_out.T, every)
    full_gate = gather(w_gate, "dp")
    full_up = gather(w_up, "dp")
    full_down_t = gather(w_down.T, "dp")

    inputs = tokens.astype(f32)
    upstream = grad_out.astype(f32) * valid_rows
    upstream_low = upstream.astype(bf16)
    ups = [upstream_low] + [swap(upstream_low, r) for r in range(1, ctx)]

    normed_f, factor_in = rms_scale(inputs, full_gain_in)
    normed = normed_f.astype(bf16)
    kv_raw = mdot(normed, full_kv)
    key_raw = kv_raw[:, : KVH * HD].reshape(rows, KVH, HD)
    value_low = kv_raw[:, KVH * HD :].astype(bf16)
    query_raw = mdot(normed, full_query).reshape(rows, H, HD)
    gain_query = full_qk[:HD]
    gain_key = full_qk[HD:]
    key_normed, factor_key = rms_scale(key_raw, gain_key)
    key_low = rotate(key_normed, cosine_table, sine_table).astype(bf16).reshape(rows, KVH * HD)
    kv_own = jnp.stack([key_low, value_low])
    kv_blocks = [kv_own] + [up(kv_own, k) for k in range(1, ctx)]
    query_normed, factor_query = rms_scale(query_raw, gain_query)
    query_low = rotate(query_normed, cosine_table, sine_table).astype(bf16)
    query_low = (query_low * (HD**-0.5)).astype(bf16).reshape(rows, H * HD)

    mixed_low, logs = attn_forward(where, query_low, kv_blocks)
    hidden = inputs + mdot(mixed_low, full_out_t, NT)
    normed_mid_f, factor_mid = rms_scale(hidden, full_gain_mid)
    normed_mid = normed_mid_f.astype(bf16)

    mids = [normed_mid] + [swap(normed_mid, r) for r in range(1, ctx)]
    kept = []
    downs, grads_mid = [], []
    for r in range(ctx):
        gate_proj = mdot(mids[r], full_gate)
        up_proj = mdot(mids[r], full_up)
        grad_activated = mdot(ups[r], full_down_t)
        gate_sigmoid = jax.nn.sigmoid(gate_proj)
        silu_gate = gate_proj * gate_sigmoid
        activated = (silu_gate * up_proj).astype(bf16)
        silu_slope = gate_sigmoid * (1.0 + gate_proj * (1.0 - gate_sigmoid))
        grad_gate = (grad_activated * up_proj * silu_slope).astype(bf16)
        grad_up = (grad_activated * silu_gate).astype(bf16)
        kept.append((activated, grad_gate, grad_up))
        grad_term = mdot(grad_gate, full_gate, NT) + mdot(grad_up, full_up, NT)
        down_term = mdot(activated, full_down_t, NT)
        if r:
            grad_term = swap(grad_term.astype(bf16), r).astype(f32)
            down_term = swap(down_term.astype(bf16), r).astype(f32)
        grads_mid.append(grad_term)
        downs.append(down_term)
    grad_mid_term = sum(grads_mid[1:], grads_mid[0])
    output = (hidden + sum(downs[1:], downs[0])).astype(bf16)

    TN = (((0,), (0,)), ((), ()))
    all_mid = jnp.concatenate(mids, 0)
    all_up = jnp.concatenate(ups, 0)
    all_act, all_gg, all_gu = (jnp.concatenate([k[i] for k in kept], 0) for i in range(3))
    grad_wgate = scatter(mdot(all_mid, all_gg, TN).astype(bf16), "dp").astype(f32)
    grad_wup = scatter(mdot(all_mid, all_gu, TN).astype(bf16), "dp").astype(f32)
    grad_wdown = scatter(mdot(all_up, all_act, TN).astype(bf16), "dp").astype(f32).T

    grad_hidden_norm, gain_terms_mid = norm_back(grad_mid_term, hidden, factor_mid, full_gain_mid)
    grad_hidden = upstream + grad_hidden_norm
    grad_branch = grad_hidden.astype(bf16)
    grad_mixed = mdot(grad_branch, full_out_t).astype(bf16)
    grad_wout_t = mdot(grad_branch, mixed_low, TN).astype(bf16)

    grad_query_rot, grad_kv_own, *grad_kv_terms = attn_backward(
        where, query_low, kv_blocks, grad_mixed, mixed_low, logs
    )
    grad_kv = grad_kv_own
    for k in range(1, ctx):
        grad_kv = grad_kv + down(grad_kv_terms[k - 1], k).astype(f32)

    grad_query_norm = rotate_back(grad_query_rot.reshape(rows, H, HD), cosine_table, sine_table)
    grad_query_raw, gain_terms_query = norm_back(
        grad_query_norm, query_raw, factor_query, gain_query
    )
    grad_key_norm = rotate_back(grad_kv[0].reshape(rows, KVH, HD), cosine_table, sine_table)
    grad_key_raw, gain_terms_key = norm_back(grad_key_norm, key_raw, factor_key, gain_key)
    grad_query_low = grad_query_raw.reshape(rows, H * HD).astype(bf16)
    grad_kv_low = jnp.concatenate(
        [grad_key_raw.reshape(rows, KVH * HD).astype(bf16), grad_kv[1].astype(bf16)], 1
    )
    grad_wquery = mdot(normed, grad_query_low, TN).astype(bf16)
    grad_wkv = mdot(normed, grad_kv_low, TN).astype(bf16)
    grad_normed = mdot(grad_query_low, full_query, NT) + mdot(grad_kv_low, full_kv, NT)
    grad_input_norm, gain_terms_in = norm_back(grad_normed, inputs, factor_in, full_gain_in)
    grad_tokens = grad_hidden + grad_input_norm
    grad_qk = jnp.concatenate(
        [jnp.sum(gain_terms_query, axis=(0, 1)), jnp.sum(gain_terms_key, axis=(0, 1))]
    )
    qk_column = jnp.pad(grad_qk.reshape(world, qk_share), ((0, 0), (0, share - qk_share)))
    grad_extra = jnp.stack(
        [jnp.sum(gain_terms_in, axis=0), jnp.sum(gain_terms_mid, axis=0), qk_column.reshape(-1)], 1
    )
    grad_extra = jnp.pad(grad_extra, ((0, 0), (0, 125))).astype(bf16)
    grad_wout = scatter(grad_wout_t, every).astype(f32).T
    grad_rest = scatter(jnp.concatenate([grad_wquery, grad_wkv, grad_extra], 1), every).astype(f32)
    cuts = (H * HD, H * HD + KVH * HD, H * HD + 2 * KVH * HD)
    return (
        output,
        grad_tokens,
        grad_rest[:, cuts[2]],
        grad_rest[:, : cuts[0]],
        grad_rest[:, cuts[0] : cuts[1]],
        grad_rest[:, cuts[1] : cuts[2]],
        grad_wout,
        grad_rest[:qk_share, cuts[2] + 2],
        grad_rest[:, cuts[2] + 1],
        grad_wgate,
        grad_wup,
        grad_wdown,
    )


def solution(mesh):
    every = ("dp", "ctx")
    rows, one = P(every, None), P(every)
    in_specs = (
        rows,
        P("dp"),
        one,
        rows,
        rows,
        rows,
        P(None, every),
        one,
        one,
        P("dp", "ctx"),
        P("dp", "ctx"),
        P("ctx", "dp"),
        rows,
    )
    out_specs = (
        rows,
        rows,
        one,
        rows,
        rows,
        rows,
        P(None, every),
        one,
        one,
        P("dp", "ctx"),
        P("dp", "ctx"),
        P("ctx", "dp"),
    )
    return jax.shard_map(shards, mesh=mesh, in_specs=in_specs, out_specs=out_specs, check_vma=False)
```

```python
import functools

import jax
import jax.numpy as jnp
from jax import lax
from jax.experimental import pallas as pl
from jax.experimental.pallas import tpu as pltpu
from jax.sharding import PartitionSpec as P

H = 24
KVH = 8
HD = 64
GROUP = H // KVH
PAIRS = KVH // 2


EPSILON = 1e-05
THETA = 1000000.0
NEG_BIG = -1e30

f32 = jnp.float32
bf16 = jnp.bfloat16

NT = (((1,), (1,)), ((), ()))
NN = (((1,), (0,)), ((), ()))
TN = (((0,), (0,)), ((), ()))


def rms_scale(values, gain_vec):
    factor = lax.rsqrt(jnp.mean(values * values, axis=-1, keepdims=True) + EPSILON)
    return (values * factor * gain_vec, factor)


def norm_back(grad_upper, values, factor, gain_vec):
    unit_rows = values * factor
    scaled = grad_upper * gain_vec
    grad_lower = factor * (
        scaled - unit_rows * jnp.mean(scaled * unit_rows, axis=-1, keepdims=True)
    )
    return (grad_lower, grad_upper * unit_rows)


def rope_tables(positions, head_width):
    half_width = head_width // 2
    frequency = THETA ** (-jnp.arange(half_width, dtype=jnp.float32) * 2.0 / head_width)
    angles = positions.astype(jnp.float32)[:, None] * frequency[None, :]
    cosine_table = jnp.concatenate([jnp.cos(angles), jnp.cos(angles)], -1)[:, None, :]
    sine_table = jnp.concatenate([jnp.sin(angles), jnp.sin(angles)], -1)[:, None, :]
    return (cosine_table, sine_table)


def rotate(values, cosine_table, sine_table):
    half_width = values.shape[-1] // 2
    turned = jnp.concatenate([-values[..., half_width:], values[..., :half_width]], -1)
    return values * cosine_table + turned * sine_table


def rotate_back(grad_upper, cosine_table, sine_table):
    half_width = grad_upper.shape[-1] // 2
    moved_sine = grad_upper * sine_table
    turned = jnp.concatenate([moved_sine[..., half_width:], -moved_sine[..., :half_width]], -1)
    return grad_upper * cosine_table + turned


def mdot(a, b, dims=NN):
    return lax.dot_general(a, b, dims, preferred_element_type=f32)


ANY = pl.BlockSpec(memory_space=pl.ANY)


def remote(src, dst, send, recv, dp, ctx):
    return pltpu.make_async_remote_copy(
        src_ref=src,
        dst_ref=dst,
        send_sem=send,
        recv_sem=recv,
        device_id=(dp, ctx),
        device_id_type=pl.DeviceIdType.MESH,
    )


def greet(dp, ctx, near, far):
    barrier = pltpu.get_barrier_semaphore()
    partners = [(dp ^ r, ctx) for r in near] + [(dp, ctx ^ s) for s in far]
    for partner in partners:
        pl.semaphore_signal(
            barrier, inc=1, device_id=partner, device_id_type=pl.DeviceIdType.MESH
        )
    pl.semaphore_wait(barrier, len(partners))


def gather_kernel(parts, riders, *refs):
    srcs, riding = refs[:parts], refs[parts : parts + riders]
    outs, landed = refs[parts + riders : 2 * parts + riders], refs[2 * parts + riders :][:riders]
    own_sem, send, recv, ride_send, ride_recv = refs[2 * parts + 2 * riders :]
    dp, ctx = lax.axis_index("dp"), lax.axis_index("ctx")
    greet(dp, ctx, (1, 2, 4), (1, 2, 3))

    def ride(i):
        return remote(riding[i], landed[i], ride_send.at[i], ride_recv.at[i], dp, ctx ^ 1)

    def line(p, s):
        return remote(
            srcs[p], outs[p].at[dp, ctx], send.at[p, s - 1], recv.at[p, s - 1], dp, ctx ^ s
        )

    def plane(p, way):
        return remote(
            outs[p].at[dp], outs[p].at[dp], send.at[p, 3 + way], recv.at[p, 3 + way],
            dp ^ (2 << way), ctx,
        )

    def corner(p, way):
        block = outs[p].at[dp ^ (2 << (1 - way)), pl.ds(2 * way, 2)]
        return remote(block, block, send.at[p, 5 + way], recv.at[p, 5 + way], dp ^ (2 << way), ctx)

    def across(p, k):
        block = outs[p].at[dp ^ (2 * k)]
        return remote(block, block, send.at[p, 7 + k], recv.at[p, 7 + k], dp ^ 1, ctx)

    def own(p):
        return pltpu.make_async_copy(srcs[p], outs[p].at[dp, ctx], own_sem.at[p])

    for p in range(parts):
        own(p).start()
        for s in (1, 2, 3):
            line(p, s).start()
    for i in range(riders):
        ride(i).start()
    for step in range(parts + 2):
        if step < parts:
            p = step
            own(p).wait()
            for s in (1, 2, 3):
                line(p, s).wait_recv()
            for way in (0, 1):
                plane(p, way).start()
            across(p, 0).start()
        if 0 <= step - 1 < parts:
            p = step - 1
            for way in (0, 1):
                plane(p, way).wait_recv()
            for way in (0, 1):
                corner(p, way).start()
            for k in (1, 2):
                across(p, k).start()
        if 0 <= step - 2 < parts:
            p = step - 2
            for way in (0, 1):
                corner(p, way).wait_recv()
            across(p, 3).start()
    for p in range(parts):
        for s in (1, 2, 3):
            line(p, s).wait_send()
        for way in (0, 1):
            plane(p, way).wait_send()
            corner(p, way).wait_send()
        for k in range(4):
            across(p, k).wait_send()
            across(p, k).wait_recv()
    for i in range(riders):
        ride(i).wait()


def gather_all(shards, riding, cid):
    parts, riders = len(shards), len(riding)
    outs = pl.pallas_call(
        functools.partial(gather_kernel, parts, riders),
        in_specs=[ANY] * (parts + riders),
        out_specs=[ANY] * (parts + riders),
        out_shape=[jax.ShapeDtypeStruct((8, 4) + s.shape, s.dtype) for s in shards]
        + [jax.ShapeDtypeStruct(s.shape, s.dtype) for s in riding],
        scratch_shapes=[
            pltpu.SemaphoreType.DMA((parts,)),
            pltpu.SemaphoreType.DMA((parts, 11)),
            pltpu.SemaphoreType.DMA((parts, 11)),
            pltpu.SemaphoreType.DMA((max(riders, 1),)),
            pltpu.SemaphoreType.DMA((max(riders, 1),)),
        ],
        compiler_params=pltpu.CompilerParams(collective_id=cid, has_side_effects=True),
        name="gather_all",
    )(*shards, *riding)
    full = [o.reshape(32 * s.shape[0], s.shape[1]) for o, s in zip(outs, shards)]
    return full + list(outs[parts:])


def sum_kernel(parts, *refs):
    ins, outs = refs[:parts], refs[parts : 2 * parts]
    keep = refs[2 * parts : 3 * parts]
    got = refs[3 * parts : 4 * parts]
    plane1 = refs[4 * parts : 5 * parts]
    plane2 = refs[5 * parts : 6 * parts]
    lines = refs[6 * parts : 7 * parts]
    load, send, recv = refs[7 * parts :]
    dp, ctx = lax.axis_index("dp"), lax.axis_index("ctx")
    chip = dp // 2
    core = dp - 2 * chip

    halves = (pl.ds(0, 2), pl.ds(2, 2))

    def fetch(p, k):
        return pltpu.make_async_copy(
            ins[p].at[2 * (chip ^ k) + core], keep[p].at[k], load.at[p, k]
        )

    def across(p, k):
        return remote(
            ins[p].at[2 * (chip ^ k) + (1 - core)], got[p].at[k],
            send.at[p, k], recv.at[p, k], dp ^ 1, ctx,
        )

    def first(p, w, i):
        k = (1 << w) if i == 0 else 3
        return remote(
            keep[p].at[k, halves[w]], plane1[p].at[i, halves[w]],
            send.at[p, 4 + 2 * w + i], recv.at[p, 4 + 2 * w + i], dp ^ (2 << w), ctx,
        )

    def second(p, w):
        k = 1 << (1 - w)
        return remote(
            keep[p].at[k, halves[w]], plane2[p].at[halves[w]],
            send.at[p, 8 + w], recv.at[p, 8 + w], dp ^ (2 << (1 - w)), ctx,
        )

    def line(p, s):
        return remote(
            keep[p].at[0, ctx ^ s], lines[p].at[s - 1],
            send.at[p, 9 + s], recv.at[p, 9 + s], dp, ctx ^ s,
        )

    for p in range(parts):
        for k in (3, 1, 2, 0):
            fetch(p, k).start()
    greet(dp, ctx, (1, 2, 4), (1, 2, 3))
    for p in range(parts):
        for k in (3, 1, 2, 0):
            across(p, k).start()

    def add(target, term):
        target[...] = (target[...].astype(f32) + term[...].astype(f32)).astype(bf16)

    for step in range(parts + 3):
        if step < parts:
            p = step
            for k in (3, 1, 2, 0):
                fetch(p, k).wait()
                across(p, k).wait_recv()
                for c in range(4):
                    add(keep[p].at[k, c], got[p].at[k, c])
                if k == 3:
                    for w in (0, 1):
                        first(p, w, 1).start()
                elif k:
                    first(p, k - 1, 0).start()
        if 0 <= step - 1 < parts:
            p = step - 1
            for w in (0, 1):
                first(p, w, 1).wait_recv()
                other = 1 << (1 - w)
                for c in (2 * w, 2 * w + 1):
                    add(keep[p].at[other, c], plane1[p].at[1, c])
                second(p, w).start()
            for w in (0, 1):
                first(p, w, 0).wait_recv()
                for c in (2 * w, 2 * w + 1):
                    add(keep[p].at[0, c], plane1[p].at[0, c])
        if 0 <= step - 2 < parts:
            p = step - 2
            for w in (0, 1):
                second(p, w).wait_recv()
                for c in (2 * w, 2 * w + 1):
                    add(keep[p].at[0, c], plane2[p].at[c])
            for s in (3, 2, 1):
                line(p, s).start()
        if 0 <= step - 3 < parts:
            p = step - 3
            for s in (1, 2, 3):
                line(p, s).wait_recv()
            total = keep[p][0, ctx].astype(f32)
            for s in (1, 2, 3):
                total = total + lines[p][s - 1].astype(f32)
            outs[p][...] = total
    for p in range(parts):
        for k in range(4):
            across(p, k).wait_send()
        for w in (0, 1):
            for i in (0, 1):
                first(p, w, i).wait_send()
            second(p, w).wait_send()
        for s in (1, 2, 3):
            line(p, s).wait_send()


def sum_all(terms, cid):
    parts = len(terms)
    blocks = [t.reshape(8, 4, t.shape[0] // 32, t.shape[1]) for t in terms]
    shapes = [b.shape[2:] for b in blocks]

    def per(lead):
        return [pltpu.VMEM(lead + s, bf16) for s in shapes]

    return pl.pallas_call(
        functools.partial(sum_kernel, parts),
        in_specs=[ANY] * parts,
        out_specs=[pl.BlockSpec(memory_space=pltpu.VMEM)] * parts,
        out_shape=[jax.ShapeDtypeStruct(s, f32) for s in shapes],
        scratch_shapes=per((4, 4)) + per((4, 4)) + per((2, 4)) + per((4,)) + per((3,))
        + [
            pltpu.SemaphoreType.DMA((parts, 4)),
            pltpu.SemaphoreType.DMA((parts, 13)),
            pltpu.SemaphoreType.DMA((parts, 13)),
        ],
        compiler_params=pltpu.CompilerParams(
            collective_id=cid, has_side_effects=True, vmem_limit_bytes=48 * 2**20
        ),
        name="sum_all",
    )(*blocks)


def causal_mask(rows, limit, key_axis):
    shape = (rows, rows)
    key = lax.broadcasted_iota(jnp.int32, shape, key_axis)
    row = lax.broadcasted_iota(jnp.int32, shape, 1 - key_axis)
    return jnp.where((key <= row) & (key < limit), 0.0, NEG_BIG).astype(f32)


def attn_fwd_kernel(blocks, where_ref, q_ref, *refs):
    kv_refs, (o_ref, log_ref, mask, acc) = refs[:blocks], refs[blocks:]
    rows = q_ref.shape[0]
    mine, limit = where_ref[0], where_ref[1]

    @pl.when(pl.program_id(0) == 0)
    def _():
        mask[...] = causal_mask(rows, limit, 1)

    def head(kv_ref, pair, diagonal):
        keys = kv_ref[0][:, pair * HD : (pair + 1) * HD]
        values = kv_ref[1][:, pair * HD : (pair + 1) * HD]
        extended = jnp.concatenate([values, jnp.ones_like(values)], -1)
        for g in range(GROUP):
            h = pair * GROUP + g
            scores = mdot(q_ref[:, h * HD : (h + 1) * HD], keys, NT)
            if diagonal:
                scores = scores + mask[...]
            term = mdot(jnp.exp(scores).astype(bf16), extended)
            acc[h] = term if diagonal else acc[h] + term

    for pair in range(2):
        head(kv_refs[0], pair, True)
    for back in range(1, blocks):

        @pl.when(mine >= back)
        def _():
            for pair in range(2):
                head(kv_refs[back], pair, False)

    lane = lax.broadcasted_iota(jnp.int32, (rows, 2 * HD), 1)
    logs = jnp.zeros((rows, 2 * HD), f32)
    for h in range(2 * GROUP):
        full = acc[h]
        total = full[:, HD : HD + 1]
        o_ref[:, h * HD : (h + 1) * HD] = (full[:, :HD] / total).astype(bf16)
        logs = jnp.where(lane == h, jnp.log(total), logs)
    log_ref[0] = jnp.transpose(logs)[:8]


def attn_bwd_kernel(blocks, where_ref, q_ref, *refs):
    kv_refs = refs[:blocks]
    do_ref, o_ref, log_ref = refs[blocks : blocks + 3]
    dq_ref = refs[blocks + 3]
    dkv_refs = refs[blocks + 4 : 2 * blocks + 4]
    mask, dqt, inner = refs[2 * blocks + 4 :]
    rows = q_ref.shape[0]
    mine, limit = where_ref[0], where_ref[1]

    @pl.when(pl.program_id(0) == 0)
    def _():
        mask[...] = causal_mask(rows, limit, 0)

    ones = jnp.ones((8, HD), f32)
    for h in range(2 * GROUP):
        cols = slice(h * HD, (h + 1) * HD)
        product = do_ref[:, cols].astype(f32) * o_ref[:, cols].astype(f32)
        inner[h] = lax.dot_general(
            ones, product, NT, preferred_element_type=f32, precision=lax.Precision.HIGHEST
        )

    def head(back, pair):
        cols = slice(pair * HD, (pair + 1) * HD)
        keys = kv_refs[back][0][:, cols]
        values = kv_refs[back][1][:, cols]
        keys_t = jnp.transpose(keys)
        grad_k = jnp.zeros((rows, HD), f32)
        grad_v = jnp.zeros((rows, HD), f32)
        for g in range(GROUP):
            h = pair * GROUP + g
            query = q_ref[:, h * HD : (h + 1) * HD]
            grad = do_ref[:, h * HD : (h + 1) * HD]
            scores = mdot(keys, query, NT) - log_ref[0][h : h + 1]
            if back == 0:
                scores = scores + mask[...]
            probs = jnp.exp(scores)
            gaps = mdot(values, grad, NT) - inner[h][0:1]
            grad_scores = (probs * gaps).astype(bf16)
            grad_k += mdot(grad_scores, query)
            grad_v += mdot(probs.astype(bf16), grad)
            term = mdot(keys_t, grad_scores)
            dqt[h] = term if back == 0 else dqt[h] + term
        dkv_refs[back][0, :, cols] = grad_k.astype(dkv_refs[back].dtype)
        dkv_refs[back][1, :, cols] = grad_v.astype(dkv_refs[back].dtype)

    for pair in range(2):
        head(0, pair)
    for back in range(1, blocks):

        @pl.when(mine >= back)
        def _():
            for pair in range(2):
                head(back, pair)

        @pl.when(mine < back)
        def _():
            dkv_refs[back][...] = jnp.zeros_like(dkv_refs[back])

    for h in range(2 * GROUP):
        dq_ref[:, h * HD : (h + 1) * HD] = jnp.transpose(dqt[h]) * (HD**-0.5)


def kv_spec(rows):
    return pl.BlockSpec((2, rows, 2 * HD), lambda i, *_: (0, 0, i))


def head_spec(rows):
    return pl.BlockSpec((rows, 2 * GROUP * HD), lambda i, *_: (0, i))


def log_spec(rows):
    return pl.BlockSpec((1, 8, rows), lambda i, *_: (i, 0, 0))


def attn_forward(where, query, kv_blocks):
    rows, blocks = query.shape[0], len(kv_blocks)
    return pl.pallas_call(
        functools.partial(attn_fwd_kernel, blocks),
        grid_spec=pltpu.PrefetchScalarGridSpec(
            num_scalar_prefetch=1,
            grid=(PAIRS,),
            in_specs=[head_spec(rows)] + [kv_spec(rows)] * blocks,
            out_specs=[head_spec(rows), log_spec(rows)],
            scratch_shapes=[
                pltpu.VMEM((rows, rows), f32),
                pltpu.VMEM((2 * GROUP, rows, 2 * HD), f32),
            ],
        ),
        out_shape=[
            jax.ShapeDtypeStruct((rows, H * HD), bf16),
            jax.ShapeDtypeStruct((PAIRS, 8, rows), f32),
        ],
        compiler_params=pltpu.CompilerParams(vmem_limit_bytes=48 * 2**20),
        name="attn_forward",
    )(where, query, *kv_blocks)


def attn_backward(where, query, kv_blocks, grad, mixed, logs):
    rows, blocks = query.shape[0], len(kv_blocks)
    kinds = [f32] + [bf16] * (blocks - 1)
    return pl.pallas_call(
        functools.partial(attn_bwd_kernel, blocks),
        grid_spec=pltpu.PrefetchScalarGridSpec(
            num_scalar_prefetch=1,
            grid=(PAIRS,),
            in_specs=[head_spec(rows)]
            + [kv_spec(rows)] * blocks
            + [head_spec(rows), head_spec(rows), log_spec(rows)],
            out_specs=[head_spec(rows)] + [kv_spec(rows)] * blocks,
            scratch_shapes=[
                pltpu.VMEM((rows, rows), f32),
                pltpu.VMEM((2 * GROUP, HD, rows), f32),
                pltpu.VMEM((2 * GROUP, 8, rows), f32),
            ],
        ),
        out_shape=[jax.ShapeDtypeStruct((rows, H * HD), f32)]
        + [jax.ShapeDtypeStruct((2, rows, KVH * HD), kind) for kind in kinds],
        compiler_params=pltpu.CompilerParams(vmem_limit_bytes=56 * 2**20),
        name="attn_backward",
    )(where, query, *kv_blocks, grad, mixed, logs)


def feed_forward_kernel(dp_blocks, *refs):
    mid_hbm, gate_hbm, up_hbm, down_hbm = refs[:4]
    ups_hbm = refs[4:8]
    grad_ref, parts_hbm, dw_hbm = refs[8:11]
    mids, ups, w_gate, w_up, w_down, act, grad_g, grad_u, to_send, received, staged = refs[11:22]
    load, store, out_sem, send, recv = refs[22:]
    rows, width = mid_hbm.shape
    hidden = gate_hbm.shape[1]
    share = width // dp_blocks
    tile, whole = 256, hidden // 256
    dp, ctx = lax.axis_index("dp"), lax.axis_index("ctx")
    middle = (ctx == 1) | (ctx == 2)

    def slot(ref, r):
        return ref.at[pl.ds(pl.multiple_of(r * rows, rows), rows)]

    def give(r):
        return remote(mid_hbm, slot(mids, r), send.at[r], recv.at[r], dp, ctx ^ r)

    relay = remote(slot(mids, 2), slot(mids, 3), send.at[0], recv.at[3], dp, ctx ^ 1)

    def back(r):
        return remote(
            to_send.at[r - 1], received.at[r - 1], send.at[3 + r], recv.at[3 + r], dp, ctx ^ r
        )

    def load_ups(r, source):
        return pltpu.make_async_copy(source, slot(ups, r), load.at[r])

    own = pltpu.make_async_copy(mid_hbm, slot(mids, 0), load.at[4])
    weights = [
        pltpu.make_async_copy(source, target, load.at[5 + i])
        for i, (source, target) in enumerate(
            ((gate_hbm, w_gate), (up_hbm, w_up), (down_hbm, w_down))
        )
    ]

    def put_down(r):
        return pltpu.make_async_copy(
            staged.at[lax.rem(r, 2)], parts_hbm.at[ctx ^ r], store.at[lax.rem(r, 2)]
        )

    own.start()
    for copy in weights:
        copy.start()
    for r in range(4):
        load_ups(r, ups_hbm[r]).start()
    greet(dp, ctx, (), (1, 2, 3))
    give(1).start()
    give(2).start()

    @pl.when(middle)
    def _():
        give(3).start()

    own.wait()
    for copy in weights:
        copy.wait()

    def block(r, carry):
        @pl.when(r > 0)
        def _():
            give(r).wait_recv()

        @pl.when((r == 2) & middle)
        def _():
            relay.start()

        load_ups(r, mid_hbm).wait()
        here = pl.ds(pl.multiple_of(r * rows, rows), rows)

        def activate(cols):
            value, upper = mids[here, :], ups[here, :]
            gate_proj = mdot(value, w_gate[:, cols])
            up_proj = mdot(value, w_up[:, cols])
            grad_activated = mdot(upper, w_down[:, cols])
            gate_sigmoid = jax.nn.sigmoid(gate_proj)
            silu_gate = gate_proj * gate_sigmoid
            silu_slope = gate_sigmoid * (1.0 + gate_proj * (1.0 - gate_sigmoid))
            act[here, cols] = (silu_gate * up_proj).astype(bf16)
            grad_g[here, cols] = (grad_activated * up_proj * silu_slope).astype(bf16)
            grad_u[here, cols] = (grad_activated * silu_gate).astype(bf16)

        def one(t, carry):
            activate(pl.ds(pl.multiple_of(t * tile, tile), tile))
            return carry

        lax.fori_loop(0, whole, one, 0)
        if hidden % tile:
            activate(pl.ds(whole * tile, hidden % tile))

        @pl.when(r >= 2)
        def _():
            put_down(r).wait()

        def two(t, carry):
            cols = pl.ds(pl.multiple_of(t * tile, tile), tile)
            term = mdot(grad_g[here, :], w_gate[cols, :], NT)
            term += mdot(grad_u[here, :], w_up[cols, :], NT)

            @pl.when(r == 0)
            def _():
                grad_ref[:, cols] = term

            @pl.when(r > 0)
            def _():
                to_send[lax.max(r - 1, 0), :, cols] = term.astype(bf16)

            staged[lax.rem(r, 2), :, cols] = mdot(act[here, :], w_down[cols, :], NT).astype(bf16)
            return carry

        lax.fori_loop(0, width // tile, two, 0)
        put_down(r).start()

        @pl.when(r > 0)
        def _():
            back(r).start()

        return carry

    lax.fori_loop(0, 4, block, 0)

    step = 384
    for i, (left, right, place) in enumerate(
        ((mids, grad_g, w_gate), (mids, grad_u, w_up), (ups, act, w_down))
    ):

        def put(j):
            return pltpu.make_async_copy(
                place.at[pl.ds(pl.multiple_of(j * share, share), share)],
                dw_hbm.at[j, i],
                out_sem.at[i, j],
            )

        def three(t, carry):
            cols = pl.ds(pl.multiple_of(t * step, step), step)
            place[cols, :] = mdot(left[:, cols], right[...], TN).astype(bf16)
            for k in range(step // share):
                put(t * (step // share) + k).start()
            return carry

        lax.fori_loop(0, width // step, three, 0)

    for r in (1, 2, 3):
        back(r).wait_recv()
        grad_ref[...] += received[r - 1].astype(f32)
    for r in (1, 2, 3):
        back(r).wait_send()
    give(1).wait_send()
    give(2).wait_send()

    @pl.when(middle)
    def _():
        give(3).wait_send()
        relay.wait_send()

    for r in (2, 3):
        put_down(r).wait()
    for i, place in enumerate((w_gate, w_up, w_down)):
        for j in range(dp_blocks):
            pltpu.make_async_copy(
                place.at[pl.ds(j * share, share)], dw_hbm.at[j, i], out_sem.at[i, j]
            ).wait()


def feed_forward(mid, ups, full_gate, full_up, full_down_t, dp_blocks, cid):
    rows, width = mid.shape
    hidden = full_gate.shape[1]
    weight = pltpu.VMEM((width, hidden), bf16)
    kept = pltpu.VMEM((4 * rows, hidden), bf16)
    every_row = pltpu.VMEM((4 * rows, width), bf16)
    return pl.pallas_call(
        functools.partial(feed_forward_kernel, dp_blocks),
        in_specs=[ANY] * 8,
        out_specs=[pl.BlockSpec(memory_space=pltpu.VMEM), ANY, ANY],
        out_shape=[
            jax.ShapeDtypeStruct((rows, width), f32),
            jax.ShapeDtypeStruct((4, rows, width), bf16),
            jax.ShapeDtypeStruct((dp_blocks, 3, width // dp_blocks, hidden), bf16),
        ],
        scratch_shapes=[every_row, every_row, weight, weight, weight, kept, kept, kept]
        + [
            pltpu.VMEM((3, rows, width), bf16),
            pltpu.VMEM((3, rows, width), bf16),
            pltpu.VMEM((2, rows, width), bf16),
            pltpu.SemaphoreType.DMA((8,)),
            pltpu.SemaphoreType.DMA((2,)),
            pltpu.SemaphoreType.DMA((3, dp_blocks)),
            pltpu.SemaphoreType.DMA((7,)),
            pltpu.SemaphoreType.DMA((7,)),
        ],
        compiler_params=pltpu.CompilerParams(
            collective_id=cid, has_side_effects=True, vmem_limit_bytes=63 * 2**20
        ),
        name="feed_forward",
    )(mid, full_gate, full_up, full_down_t, *ups)


def shards(
    tokens,
    seq_lens,
    gain_in,
    w_query,
    w_key,
    w_value,
    w_out,
    qk_gains,
    gain_mid,
    w_gate,
    w_up,
    w_down,
    grad_out,
):
    every = ("dp", "ctx")
    rows, width = tokens.shape
    ctx = lax.axis_size("ctx")
    world = ctx * lax.axis_size("dp")
    mine = lax.axis_index("ctx")
    share = w_query.shape[0]
    qk_share = qk_gains.shape[0]
    positions = mine * rows + jnp.arange(rows, dtype=jnp.int32)
    length = seq_lens[0]
    where = jnp.stack([mine.astype(jnp.int32), length - mine * rows])
    cosine_table, sine_table = rope_tables(positions, HD)

    small = (lax.axis_size("dp"), ctx) == (8, 4)

    def move(block, pairs):
        return lax.ppermute(block, "ctx", pairs)

    def lift(block):
        one = move(block, [(0, 1), (1, 2), (2, 3)])
        two = move(block, [(0, 2), (1, 3)])
        return [block, one, two, move(block, [(0, 3)])]

    def lower(terms):
        relay = move(terms[3], [(3, 2)])
        two = move((terms[2].astype(f32) + relay.astype(f32)).astype(bf16), [(2, 0), (3, 1)])
        one = move(terms[1], [(1, 0), (2, 1), (3, 2)])
        return terms[0].astype(f32) + one.astype(f32) + two.astype(f32)

    def after(value, *others):
        return lax.optimization_barrier((value, others))[0]

    def swap(block, r):
        return move(block, [(i, i ^ r) for i in range(ctx)])

    def gather(blocks, riding, cid):
        if small:
            return gather_all(blocks, riding, cid)
        full = [lax.all_gather(b, every, axis=0, tiled=True) for b in blocks]
        return full + [swap(b, 1) for b in riding]

    def collect(terms, cid):
        if small:
            return sum_all(terms, cid)
        return [
            lax.psum_scatter(t, every, scatter_dimension=0, tiled=True).astype(f32) for t in terms
        ]

    extra = jnp.stack([gain_in, gain_mid, jnp.pad(qk_gains, (0, share - qk_share))], 1)
    extra = jnp.pad(extra, ((0, 0), (0, 125)))
    valid_rows = (positions < length).astype(f32)[:, None]
    upstream = grad_out.astype(f32) * valid_rows
    upstream_low = upstream.astype(bf16)
    full_kv, full_query, full_out_t, ups_near = gather(
        [jnp.concatenate([w_key, w_value, extra], 1), w_query, w_out.T], [upstream_low], 1
    )
    kv_width = 2 * KVH * HD
    full_extra = full_kv[:, kv_width:].astype(f32)
    full_gain_in, full_gain_mid = full_extra[:, 0], full_extra[:, 1]
    full_qk = full_extra[:, 2].reshape(world, share)[:, :qk_share].reshape(-1)
    full_gate, full_up, full_down_t = (
        lax.all_gather(after(w, full_kv), "dp", axis=0, tiled=True)
        for w in (w_gate, w_up, w_down.T)
    )
    full_kv = full_kv[:, :kv_width]

    inputs = tokens.astype(f32)

    normed_f, factor_in = rms_scale(inputs, full_gain_in)
    normed = normed_f.astype(bf16)
    kv_raw = mdot(normed, full_kv)
    key_raw = kv_raw[:, : KVH * HD].reshape(rows, KVH, HD)
    value_low = kv_raw[:, KVH * HD :].astype(bf16)
    gain_query = full_qk[:HD]
    gain_key = full_qk[HD:]
    key_normed, factor_key = rms_scale(key_raw, gain_key)
    key_low = rotate(key_normed, cosine_table, sine_table).astype(bf16).reshape(rows, KVH * HD)
    kv_own = jnp.stack([key_low, value_low])
    kv_blocks = lift(kv_own)
    far_low = after(upstream_low, kv_blocks)
    ups_two = swap(far_low, 2)
    ups_middle = move(far_low, [(1, 2), (2, 1)])
    ups_ends = move(ups_two, [(2, 3), (1, 0)])
    ups_three = jnp.where((mine == 1) | (mine == 2), ups_middle, ups_ends)
    ups = [upstream_low, ups_near, ups_two, ups_three]
    query_raw = mdot(normed, full_query).reshape(rows, H, HD)
    query_normed, factor_query = rms_scale(query_raw, gain_query)
    query_low = rotate(query_normed, cosine_table, sine_table).astype(bf16)
    query_low = (query_low * (HD**-0.5)).astype(bf16).reshape(rows, H * HD)

    mixed_low, logs = attn_forward(where, query_low, kv_blocks)
    hidden = inputs + mdot(mixed_low, full_out_t, NT)
    normed_mid_f, factor_mid = rms_scale(hidden, full_gain_mid)
    normed_mid = normed_mid_f.astype(bf16)

    grad_mid_term, down_parts, grad_ffn = feed_forward(
        normed_mid, ups, full_gate, full_up, full_down_t, lax.axis_size("dp"), 2
    )
    grad_ffn = lax.psum_scatter(
        grad_ffn.reshape(-1, grad_ffn.shape[-1]), "dp", scatter_dimension=0, tiled=True
    )
    down_parts = lax.psum_scatter(
        down_parts.reshape(-1, width), "ctx", scatter_dimension=0, tiled=True
    )
    grad_hidden_norm, gain_terms_mid = norm_back(grad_mid_term, hidden, factor_mid, full_gain_mid)
    grad_hidden = upstream + grad_hidden_norm
    grad_branch = grad_hidden.astype(bf16)
    grad_mixed = mdot(grad_branch, full_out_t).astype(bf16)
    grad_wout_t = mdot(grad_branch, mixed_low, TN).astype(bf16)

    grad_query_rot, grad_kv_own, *grad_kv_terms = attn_backward(
        where, query_low, kv_blocks, grad_mixed, mixed_low, logs
    )
    grad_query_norm = rotate_back(grad_query_rot.reshape(rows, H, HD), cosine_table, sine_table)
    grad_query_raw, gain_terms_query = norm_back(
        grad_query_norm, query_raw, factor_query, gain_query
    )
    grad_query_low = grad_query_raw.reshape(rows, H * HD).astype(bf16)
    grad_wquery = mdot(normed, grad_query_low, TN).astype(bf16)
    sum_query, grad_wout = collect([grad_wquery, grad_wout_t], 3)
    grad_kv = lower([grad_kv_own] + grad_kv_terms)
    grad_key_norm = rotate_back(grad_kv[0].reshape(rows, KVH, HD), cosine_table, sine_table)
    grad_key_raw, gain_terms_key = norm_back(grad_key_norm, key_raw, factor_key, gain_key)
    grad_kv_low = jnp.concatenate(
        [grad_key_raw.reshape(rows, KVH * HD).astype(bf16), grad_kv[1].astype(bf16)], 1
    )
    grad_wkv = mdot(normed, grad_kv_low, TN).astype(bf16)
    grad_normed = mdot(grad_query_low, full_query, NT) + mdot(grad_kv_low, full_kv, NT)
    grad_input_norm, gain_terms_in = norm_back(grad_normed, inputs, factor_in, full_gain_in)
    grad_tokens = grad_hidden + grad_input_norm
    grad_qk = jnp.concatenate(
        [jnp.sum(gain_terms_query, axis=(0, 1)), jnp.sum(gain_terms_key, axis=(0, 1))]
    )
    qk_column = jnp.pad(grad_qk.reshape(world, qk_share), ((0, 0), (0, share - qk_share)))
    grad_extra = jnp.stack(
        [jnp.sum(gain_terms_in, axis=0), jnp.sum(gain_terms_mid, axis=0), qk_column.reshape(-1)], 1
    )
    grad_extra = jnp.pad(grad_extra, ((0, 0), (0, 125))).astype(bf16)
    (sum_kv,) = collect([after(jnp.concatenate([grad_wkv, grad_extra], 1), sum_query)], 4)
    grad_ffn, down_parts = after((grad_ffn, down_parts), sum_kv)
    output = (hidden + down_parts.astype(f32)).astype(bf16)
    grad_wgate, grad_wup, grad_wdown = (
        grad_ffn[i * w_gate.shape[0] : (i + 1) * w_gate.shape[0]].astype(f32) for i in range(3)
    )
    grad_wdown = grad_wdown.T
    cuts = (KVH * HD, 2 * KVH * HD)
    return (
        output,
        grad_tokens,
        sum_kv[:, cuts[1]],
        sum_query,
        sum_kv[:, : cuts[0]],
        sum_kv[:, cuts[0] : cuts[1]],
        grad_wout.T,
        sum_kv[:qk_share, cuts[1] + 2],
        sum_kv[:, cuts[1] + 1],
        grad_wgate,
        grad_wup,
        grad_wdown,
    )


def solution(mesh):
    every = ("dp", "ctx")
    rows, one = P(every, None), P(every)
    in_specs = (
        rows,
        P("dp"),
        one,
        rows,
        rows,
        rows,
        P(None, every),
        one,
        one,
        P("dp", "ctx"),
        P("dp", "ctx"),
        P("ctx", "dp"),
        rows,
    )
    out_specs = (
        rows,
        rows,
        one,
        rows,
        rows,
        rows,
        P(None, every),
        one,
        one,
        P("dp", "ctx"),
        P("dp", "ctx"),
        P("ctx", "dp"),
    )
    return jax.shard_map(shards, mesh=mesh, in_specs=in_specs, out_specs=out_specs, check_vma=False)
```

```python
import functools

import jax
import jax.numpy as jnp
from jax import lax
from jax.experimental import pallas as pl
from jax.experimental.pallas import tpu as pltpu
from jax.sharding import PartitionSpec as P

H = 24
KVH = 8
HD = 64
GROUP = H // KVH
PAIRS = KVH // 2


EPSILON = 1e-05
THETA = 1000000.0
NEG_BIG = -1e30

f32 = jnp.float32
bf16 = jnp.bfloat16

NT = (((1,), (1,)), ((), ()))
NN = (((1,), (0,)), ((), ()))
TN = (((0,), (0,)), ((), ()))


def rms_scale(values, gain_vec):
    factor = lax.rsqrt(jnp.mean(values * values, axis=-1, keepdims=True) + EPSILON)
    return (values * factor * gain_vec, factor)


def norm_back(grad_upper, values, factor, gain_vec):
    unit_rows = values * factor
    scaled = grad_upper * gain_vec
    grad_lower = factor * (
        scaled - unit_rows * jnp.mean(scaled * unit_rows, axis=-1, keepdims=True)
    )
    return (grad_lower, grad_upper * unit_rows)


def rope_tables(positions, head_width):
    half_width = head_width // 2
    frequency = THETA ** (-jnp.arange(half_width, dtype=jnp.float32) * 2.0 / head_width)
    angles = positions.astype(jnp.float32)[:, None] * frequency[None, :]
    cosine_table = jnp.concatenate([jnp.cos(angles), jnp.cos(angles)], -1)[:, None, :]
    sine_table = jnp.concatenate([jnp.sin(angles), jnp.sin(angles)], -1)[:, None, :]
    return (cosine_table, sine_table)


def rotate(values, cosine_table, sine_table):
    half_width = values.shape[-1] // 2
    turned = jnp.concatenate([-values[..., half_width:], values[..., :half_width]], -1)
    return values * cosine_table + turned * sine_table


def rotate_back(grad_upper, cosine_table, sine_table):
    half_width = grad_upper.shape[-1] // 2
    moved_sine = grad_upper * sine_table
    turned = jnp.concatenate([moved_sine[..., half_width:], -moved_sine[..., :half_width]], -1)
    return grad_upper * cosine_table + turned


def mdot(a, b, dims=NN):
    return lax.dot_general(a, b, dims, preferred_element_type=f32)


ANY = pl.BlockSpec(memory_space=pl.ANY)


def lasting(micros):
    return pl.CostEstimate(flops=micros * 10**9, bytes_accessed=0, transcendentals=0)


def remote(src, dst, send, recv, dp, ctx):
    return pltpu.make_async_remote_copy(
        src_ref=src,
        dst_ref=dst,
        send_sem=send,
        recv_sem=recv,
        device_id=(dp, ctx),
        device_id_type=pl.DeviceIdType.MESH,
    )


def greet(dp, ctx, near, far):
    barrier = pltpu.get_barrier_semaphore()
    partners = [(dp ^ r, ctx) for r in near] + [(dp, ctx ^ s) for s in far]
    for partner in partners:
        pl.semaphore_signal(
            barrier, inc=1, device_id=partner, device_id_type=pl.DeviceIdType.MESH
        )
    pl.semaphore_wait(barrier, len(partners))


def gather_kernel(parts, riders, *refs):
    srcs, riding = refs[:parts], refs[parts : parts + riders]
    outs, landed = refs[parts + riders : 2 * parts + riders], refs[2 * parts + riders :][:riders]
    own_sem, send, recv, ride_send, ride_recv = refs[2 * parts + 2 * riders :]
    dp, ctx = lax.axis_index("dp"), lax.axis_index("ctx")
    greet(dp, ctx, (1, 2, 4), (1, 2, 3))

    def ride(i):
        return remote(riding[i], landed[i], ride_send.at[i], ride_recv.at[i], dp, ctx ^ 1)

    def line(p, s):
        return remote(
            srcs[p], outs[p].at[dp, ctx], send.at[p, s - 1], recv.at[p, s - 1], dp, ctx ^ s
        )

    def plane(p, way):
        return remote(
            outs[p].at[dp], outs[p].at[dp], send.at[p, 3 + way], recv.at[p, 3 + way],
            dp ^ (2 << way), ctx,
        )

    def corner(p, way):
        block = outs[p].at[dp ^ (2 << (1 - way)), pl.ds(2 * way, 2)]
        return remote(block, block, send.at[p, 5 + way], recv.at[p, 5 + way], dp ^ (2 << way), ctx)

    def across(p, k):
        block = outs[p].at[dp ^ (2 * k)]
        return remote(block, block, send.at[p, 7 + k], recv.at[p, 7 + k], dp ^ 1, ctx)

    def own(p):
        return pltpu.make_async_copy(srcs[p], outs[p].at[dp, ctx], own_sem.at[p])

    for p in range(parts):
        own(p).start()
        for s in (1, 2, 3):
            line(p, s).start()
    for i in range(riders):
        ride(i).start()
    for step in range(parts + 2):
        if step < parts:
            p = step
            own(p).wait()
            for s in (1, 2, 3):
                line(p, s).wait_recv()
            for way in (0, 1):
                plane(p, way).start()
            across(p, 0).start()
        if 0 <= step - 1 < parts:
            p = step - 1
            for way in (0, 1):
                plane(p, way).wait_recv()
            for way in (0, 1):
                corner(p, way).start()
            for k in (1, 2):
                across(p, k).start()
        if 0 <= step - 2 < parts:
            p = step - 2
            for way in (0, 1):
                corner(p, way).wait_recv()
            across(p, 3).start()
    for p in range(parts):
        for s in (1, 2, 3):
            line(p, s).wait_send()
        for way in (0, 1):
            plane(p, way).wait_send()
            corner(p, way).wait_send()
        for k in range(4):
            across(p, k).wait_send()
            across(p, k).wait_recv()
    for i in range(riders):
        ride(i).wait()


def gather_all(shards, riding, cid):
    parts, riders = len(shards), len(riding)
    outs = pl.pallas_call(
        functools.partial(gather_kernel, parts, riders),
        in_specs=[ANY] * (parts + riders),
        out_specs=[ANY] * (parts + riders),
        out_shape=[jax.ShapeDtypeStruct((8, 4) + s.shape, s.dtype) for s in shards]
        + [jax.ShapeDtypeStruct(s.shape, s.dtype) for s in riding],
        scratch_shapes=[
            pltpu.SemaphoreType.DMA((parts,)),
            pltpu.SemaphoreType.DMA((parts, 11)),
            pltpu.SemaphoreType.DMA((parts, 11)),
            pltpu.SemaphoreType.DMA((max(riders, 1),)),
            pltpu.SemaphoreType.DMA((max(riders, 1),)),
        ],
        compiler_params=pltpu.CompilerParams(collective_id=cid, has_side_effects=True),
        name="gather_all",
    )(*shards, *riding)
    full = [o.reshape(32 * s.shape[0], s.shape[1]) for o, s in zip(outs, shards)]
    return full + list(outs[parts:])


def sum_kernel(parts, hops, *refs):
    riders = len(hops)
    ins, riding = refs[:parts], refs[parts : parts + riders]
    refs = refs[parts + riders :]
    outs, landed = refs[:parts], refs[parts : parts + riders]
    refs = refs[parts + riders :]
    keep, got, plane1, plane2, lines = (refs[i * parts : (i + 1) * parts] for i in range(5))
    load, send, recv, ride_send, ride_recv = refs[5 * parts :]
    dp, ctx = lax.axis_index("dp"), lax.axis_index("ctx")

    def ride(i):
        return remote(riding[i], landed[i], ride_send.at[i], ride_recv.at[i], dp, ctx ^ hops[i])

    chip = dp // 2
    core = dp - 2 * chip

    halves = (pl.ds(0, 2), pl.ds(2, 2))

    def fetch(p, k):
        return pltpu.make_async_copy(
            ins[p].at[2 * (chip ^ k) + core], keep[p].at[k], load.at[p, k]
        )

    def across(p, k):
        return remote(
            ins[p].at[2 * (chip ^ k) + (1 - core)], got[p].at[k],
            send.at[p, k], recv.at[p, k], dp ^ 1, ctx,
        )

    def first(p, w, i):
        k = (1 << w) if i == 0 else 3
        return remote(
            keep[p].at[k, halves[w]], plane1[p].at[i, halves[w]],
            send.at[p, 4 + 2 * w + i], recv.at[p, 4 + 2 * w + i], dp ^ (2 << w), ctx,
        )

    def second(p, w):
        k = 1 << (1 - w)
        return remote(
            keep[p].at[k, halves[w]], plane2[p].at[halves[w]],
            send.at[p, 8 + w], recv.at[p, 8 + w], dp ^ (2 << (1 - w)), ctx,
        )

    def line(p, s):
        return remote(
            keep[p].at[0, ctx ^ s], lines[p].at[s - 1],
            send.at[p, 9 + s], recv.at[p, 9 + s], dp, ctx ^ s,
        )

    for p in range(parts):
        for k in (3, 1, 2, 0):
            fetch(p, k).start()
    greet(dp, ctx, (1, 2, 4), (1, 2, 3))
    for p in range(parts):
        for k in (3, 1, 2, 0):
            across(p, k).start()
    for i in range(riders):
        ride(i).start()

    def add(target, term):
        target[...] = (target[...].astype(f32) + term[...].astype(f32)).astype(bf16)

    for step in range(parts + 3):
        if step < parts:
            p = step
            for k in (3, 1, 2, 0):
                fetch(p, k).wait()
                across(p, k).wait_recv()
                for c in range(4):
                    add(keep[p].at[k, c], got[p].at[k, c])
                if k == 3:
                    for w in (0, 1):
                        first(p, w, 1).start()
                elif k:
                    first(p, k - 1, 0).start()
        if 0 <= step - 1 < parts:
            p = step - 1
            for w in (0, 1):
                first(p, w, 1).wait_recv()
                other = 1 << (1 - w)
                for c in (2 * w, 2 * w + 1):
                    add(keep[p].at[other, c], plane1[p].at[1, c])
                second(p, w).start()
            for w in (0, 1):
                first(p, w, 0).wait_recv()
                for c in (2 * w, 2 * w + 1):
                    add(keep[p].at[0, c], plane1[p].at[0, c])
        if 0 <= step - 2 < parts:
            p = step - 2
            for w in (0, 1):
                second(p, w).wait_recv()
                for c in (2 * w, 2 * w + 1):
                    add(keep[p].at[0, c], plane2[p].at[c])
            for s in (3, 2, 1):
                line(p, s).start()
        if 0 <= step - 3 < parts:
            p = step - 3
            for s in (1, 2, 3):
                line(p, s).wait_recv()
            total = keep[p][0, ctx].astype(f32)
            for s in (1, 2, 3):
                total = total + lines[p][s - 1].astype(f32)
            outs[p][...] = total
    for p in range(parts):
        for k in range(4):
            across(p, k).wait_send()
        for w in (0, 1):
            for i in (0, 1):
                first(p, w, i).wait_send()
            second(p, w).wait_send()
        for s in (1, 2, 3):
            line(p, s).wait_send()
    for i in range(riders):
        ride(i).wait()


def sum_all(terms, riding, hops, cid):
    parts, riders = len(terms), len(riding)
    blocks = [t.reshape(8, 4, t.shape[0] // 32, t.shape[1]) for t in terms]
    shapes = [b.shape[2:] for b in blocks]

    def per(lead):
        return [pltpu.VMEM(lead + s, bf16) for s in shapes]

    return pl.pallas_call(
        functools.partial(sum_kernel, parts, hops),
        in_specs=[ANY] * (parts + riders),
        out_specs=[pl.BlockSpec(memory_space=pltpu.VMEM)] * parts + [ANY] * riders,
        out_shape=[jax.ShapeDtypeStruct(s, f32) for s in shapes]
        + [jax.ShapeDtypeStruct(r.shape, r.dtype) for r in riding],
        scratch_shapes=per((4, 4)) + per((4, 4)) + per((2, 4)) + per((4,)) + per((3,))
        + [
            pltpu.SemaphoreType.DMA((parts, 4)),
            pltpu.SemaphoreType.DMA((parts, 13)),
            pltpu.SemaphoreType.DMA((parts, 13)),
            pltpu.SemaphoreType.DMA((riders,)),
            pltpu.SemaphoreType.DMA((riders,)),
        ],
        compiler_params=pltpu.CompilerParams(
            collective_id=cid, has_side_effects=True, vmem_limit_bytes=48 * 2**20
        ),
        name="sum_all",
    )(*blocks, *riding)


def causal_mask(rows, limit, key_axis):
    shape = (rows, rows)
    key = lax.broadcasted_iota(jnp.int32, shape, key_axis)
    row = lax.broadcasted_iota(jnp.int32, shape, 1 - key_axis)
    return jnp.where((key <= row) & (key < limit), 0.0, NEG_BIG).astype(f32)


def attn_fwd_kernel(blocks, where_ref, q_ref, *refs):
    kv_refs, (o_ref, log_ref, mask, acc) = refs[:blocks], refs[blocks:]
    rows = q_ref.shape[0]
    mine, limit = where_ref[0], where_ref[1]

    @pl.when(pl.program_id(0) == 0)
    def _():
        mask[...] = causal_mask(rows, limit, 1)

    def head(kv_ref, pair, diagonal):
        keys = kv_ref[0][:, pair * HD : (pair + 1) * HD]
        values = kv_ref[1][:, pair * HD : (pair + 1) * HD]
        extended = jnp.concatenate([values, jnp.ones_like(values)], -1)
        for g in range(GROUP):
            h = pair * GROUP + g
            scores = mdot(q_ref[:, h * HD : (h + 1) * HD], keys, NT)
            if diagonal:
                scores = scores + mask[...]
            term = mdot(jnp.exp(scores).astype(bf16), extended)
            acc[h] = term if diagonal else acc[h] + term

    for pair in range(2):
        head(kv_refs[0], pair, True)
    for back in range(1, blocks):

        @pl.when(mine >= back)
        def _():
            for pair in range(2):
                head(kv_refs[back], pair, False)

    lane = lax.broadcasted_iota(jnp.int32, (rows, 2 * HD), 1)
    logs = jnp.zeros((rows, 2 * HD), f32)
    for h in range(2 * GROUP):
        full = acc[h]
        total = full[:, HD : HD + 1]
        o_ref[:, h * HD : (h + 1) * HD] = (full[:, :HD] / total).astype(bf16)
        logs = jnp.where(lane == h, jnp.log(total), logs)
    log_ref[0] = jnp.transpose(logs)[:8]


def split_dot(values, weights, dims):
    high = values.astype(bf16)
    low = (values - high.astype(f32)).astype(bf16)
    return mdot(high, weights, dims) + mdot(low, weights, dims)


def head_means(values):
    shape = (2 * HD, 2 * HD)
    same = lax.broadcasted_iota(jnp.int32, shape, 0) // HD == (
        lax.broadcasted_iota(jnp.int32, shape, 1) // HD
    )
    return split_dot(values, jnp.where(same, 1.0 / HD, 0.0).astype(bf16), NN)


def first_half(shape):
    return lax.rem(lax.broadcasted_iota(jnp.int32, shape, 1), HD) < HD // 2


def half_swap(values):
    lower = pltpu.roll(values, HD // 2, 1)
    upper = pltpu.roll(values, 2 * HD - HD // 2, 1)
    return jnp.where(first_half(values.shape), upper, lower)


def unrotate_norm_back(grad_rot, raw, cosine, signed_sine, gain):
    grad_upper = grad_rot * cosine + half_swap(grad_rot * signed_sine)
    factor = lax.rsqrt(head_means(raw * raw) + EPSILON)
    unit_rows = raw * factor
    scaled = grad_upper * gain
    grad_lower = factor * (scaled - unit_rows * head_means(scaled * unit_rows))
    return grad_lower, jnp.sum(grad_upper * unit_rows, axis=0, keepdims=True)


def attn_bwd_kernel(blocks, length_ref, q_ref, *refs):
    kv_refs = refs[:blocks]
    do_ref, o_ref, log_ref, q_raw, k_raw, cosine, sine, gains = refs[blocks : blocks + 8]
    gq_ref, gkv_ref, gain_ref = refs[blocks + 8 : blocks + 11]
    mask, dqt, inner, own, to_send, received, send, recv = refs[blocks + 11 :]
    rows = q_ref.shape[0]
    step = pl.program_id(0)
    dp, mine = lax.axis_index("dp"), lax.axis_index("ctx")

    def give(back, i):
        return remote(
            to_send.at[back - 1, i], received.at[back - 1, i],
            send.at[back - 1, i], recv.at[back - 1, i], dp, mine - back,
        )

    @pl.when(step == 0)
    def _():
        greet(dp, mine, (), (1, 2, 3))
        mask[...] = causal_mask(rows, length_ref[0] - mine * rows, 0)
        gain_ref[...] = jnp.zeros_like(gain_ref)

    ones = jnp.ones((8, HD), bf16)
    for h in range(2 * GROUP):
        cols = slice(h * HD, (h + 1) * HD)
        product = do_ref[:, cols].astype(f32) * o_ref[:, cols].astype(f32)
        high = product.astype(bf16)
        low = (product - high.astype(f32)).astype(bf16)
        inner[h] = mdot(ones, high, NT) + mdot(ones, low, NT)

    def head(back, pair):
        cols = slice(pair * HD, (pair + 1) * HD)
        keys = kv_refs[back][0][:, cols]
        values = kv_refs[back][1][:, cols]
        keys_t = jnp.transpose(keys)
        grad_k = jnp.zeros((rows, HD), f32)
        grad_v = jnp.zeros((rows, HD), f32)
        for g in range(GROUP):
            h = pair * GROUP + g
            query = q_ref[:, h * HD : (h + 1) * HD]
            grad = do_ref[:, h * HD : (h + 1) * HD]
            scores = mdot(keys, query, NT) - log_ref[0][h : h + 1]
            if back == 0:
                scores = scores + mask[...]
            probs = jnp.exp(scores)
            gaps = mdot(values, grad, NT) - inner[h][0:1]
            grad_scores = (probs * gaps).astype(bf16)
            grad_k += mdot(grad_scores, query)
            grad_v += mdot(probs.astype(bf16), grad)
            term = mdot(keys_t, grad_scores)
            dqt[h] = term if back == 0 else dqt[h] + term
        if back == 0:
            own[step, 0, :, cols] = grad_k
            own[step, 1, :, cols] = grad_v
        else:
            to_send[back - 1, step, 0, :, cols] = grad_k.astype(bf16)
            to_send[back - 1, step, 1, :, cols] = grad_v.astype(bf16)

    def hand_over(i):
        return remote(
            to_send.at[2, i], received.at[2, i], send.at[2, i], recv.at[2, i], dp, mine - 1
        )

    def pass_on(i):
        hand_over(i).wait_recv()
        for part in range(2):
            joined = to_send[1, i, part].astype(f32) + received[2, i, part].astype(f32)
            to_send[1, i, part] = joined.astype(bf16)
        give(2, i).start()

    for pair in range(2):
        head(0, pair)
    for back in (3, 2, 1):

        @pl.when(mine >= back)
        def _():
            for pair in range(2):
                head(back, pair)
            if back == 3:
                hand_over(step).start()
            elif back == 1:
                give(1, step).start()

        if back == 2:

            @pl.when(mine == 3)
            def _():
                give(2, step).start()

    @pl.when((mine == 2) & (step > 0))
    def _():
        pass_on(step - 1)

    @pl.when((mine == 2) & (step == PAIRS - 1))
    def _():
        pass_on(step)

    for j in range(GROUP):
        cols = slice(2 * j * HD, (2 * j + 2) * HD)
        turned = jnp.concatenate([jnp.transpose(dqt[2 * j]), jnp.transpose(dqt[2 * j + 1])], 1)
        grad, gain_term = unrotate_norm_back(
            turned * (HD**-0.5), q_raw[:, cols], cosine[...], sine[...], gains[0:1, :]
        )
        gq_ref[:, cols] = grad.astype(bf16)
        gain_ref[0:1, :] += gain_term

    @pl.when(step == PAIRS - 1)
    def _():
        for back in (1, 2):

            @pl.when(mine + back < blocks)
            def _():
                for i in range(PAIRS):
                    give(back, i).wait_recv()
                    for part in range(2):
                        own[i, part] += received[back - 1, i, part].astype(f32)

        for i in range(PAIRS):
            cols = slice(2 * i * HD, (2 * i + 2) * HD)
            grad, gain_term = unrotate_norm_back(
                own[i, 0], k_raw[:, cols], cosine[...], sine[...], gains[1:2, :]
            )
            gkv_ref[:, cols] = grad.astype(bf16)
            gkv_ref[:, KVH * HD + 2 * i * HD : KVH * HD + (2 * i + 2) * HD] = own[i, 1].astype(bf16)
            gain_ref[1:2, :] += gain_term
        for back in (1, 2, 3):

            @pl.when(mine >= back)
            def _():
                for i in range(PAIRS):
                    (hand_over(i) if back == 3 else give(back, i)).wait_send()


def kv_spec(rows):
    return pl.BlockSpec((2, rows, 2 * HD), lambda i, *_: (0, 0, i))


def head_spec(rows):
    return pl.BlockSpec((rows, 2 * GROUP * HD), lambda i, *_: (0, i))


def log_spec(rows):
    return pl.BlockSpec((1, 8, rows), lambda i, *_: (i, 0, 0))


def attn_forward(where, query, kv_blocks):
    rows, blocks = query.shape[0], len(kv_blocks)
    return pl.pallas_call(
        functools.partial(attn_fwd_kernel, blocks),
        grid_spec=pltpu.PrefetchScalarGridSpec(
            num_scalar_prefetch=1,
            grid=(PAIRS,),
            in_specs=[head_spec(rows)] + [kv_spec(rows)] * blocks,
            out_specs=[head_spec(rows), log_spec(rows)],
            scratch_shapes=[
                pltpu.VMEM((rows, rows), f32),
                pltpu.VMEM((2 * GROUP, rows, 2 * HD), f32),
            ],
        ),
        out_shape=[
            jax.ShapeDtypeStruct((rows, H * HD), bf16),
            jax.ShapeDtypeStruct((PAIRS, 8, rows), f32),
        ],
        compiler_params=pltpu.CompilerParams(vmem_limit_bytes=48 * 2**20),
        name="attn_forward",
    )(where, query, *kv_blocks)


def whole_spec(*shape):
    return pl.BlockSpec(shape, lambda i, *_: (0,) * len(shape))


def attn_backward(length, query, kv_blocks, grad, mixed, logs, q_raw, k_raw, tables, gains, cid):
    rows, blocks = query.shape[0], len(kv_blocks)
    pair = (2, rows, 2 * HD)
    return pl.pallas_call(
        functools.partial(attn_bwd_kernel, blocks),
        grid=(PAIRS,),
        in_specs=[pl.BlockSpec(memory_space=pltpu.SMEM), head_spec(rows)]
        + [kv_spec(rows)] * blocks
        + [head_spec(rows), head_spec(rows), log_spec(rows), head_spec(rows)]
        + [whole_spec(rows, KVH * HD)]
        + [whole_spec(rows, 2 * HD)] * 2
        + [whole_spec(2, 2 * HD)],
        out_specs=[
            head_spec(rows),
            whole_spec(rows, 2 * KVH * HD),
            whole_spec(2, 2 * HD),
        ],
        out_shape=[
            jax.ShapeDtypeStruct((rows, H * HD), bf16),
            jax.ShapeDtypeStruct((rows, 2 * KVH * HD), bf16),
            jax.ShapeDtypeStruct((2, 2 * HD), f32),
        ],
        scratch_shapes=[
            pltpu.VMEM((rows, rows), f32),
            pltpu.VMEM((2 * GROUP, HD, rows), f32),
            pltpu.VMEM((2 * GROUP, 8, rows), f32),
            pltpu.VMEM((PAIRS,) + pair, f32),
            pltpu.VMEM((blocks - 1, PAIRS) + pair, bf16),
            pltpu.VMEM((blocks - 1, PAIRS) + pair, bf16),
            pltpu.SemaphoreType.DMA((blocks - 1, PAIRS)),
            pltpu.SemaphoreType.DMA((blocks - 1, PAIRS)),
        ],
        compiler_params=pltpu.CompilerParams(
            collective_id=cid, has_side_effects=True, vmem_limit_bytes=56 * 2**20
        ),
        cost_estimate=lasting(120),
        name="attn_backward",
    )(length, query, *kv_blocks, grad, mixed, logs, q_raw, k_raw, *tables, gains)


def feed_forward_kernel(dp_blocks, *refs):
    mid_hbm, gate_hbm, up_hbm, down_hbm = refs[:4]
    ups_hbm = refs[4:8]
    grad_ref, parts_hbm, dw_hbm = refs[8:11]
    mids, ups, w_gate, w_up, w_down, act, grad_g, grad_u, to_send, received, staged = refs[11:22]
    load, store, out_sem, send, recv = refs[22:]
    rows, width = mid_hbm.shape
    hidden = gate_hbm.shape[1]
    share = width // dp_blocks
    tile, whole = 256, hidden // 256
    dp, ctx = lax.axis_index("dp"), lax.axis_index("ctx")
    middle = (ctx == 1) | (ctx == 2)

    def slot(ref, r):
        return ref.at[pl.ds(pl.multiple_of(r * rows, rows), rows)]

    def give(r):
        return remote(mid_hbm, slot(mids, r), send.at[r], recv.at[r], dp, ctx ^ r)

    relay = remote(slot(mids, 2), slot(mids, 3), send.at[0], recv.at[3], dp, ctx ^ 1)

    def back(r):
        return remote(
            to_send.at[r - 1], received.at[r - 1], send.at[3 + r], recv.at[3 + r], dp, ctx ^ r
        )

    def load_ups(r, source):
        return pltpu.make_async_copy(source, slot(ups, r), load.at[r])

    own = pltpu.make_async_copy(mid_hbm, slot(mids, 0), load.at[4])
    weights = [
        pltpu.make_async_copy(source, target, load.at[5 + i])
        for i, (source, target) in enumerate(
            ((gate_hbm, w_gate), (up_hbm, w_up), (down_hbm, w_down))
        )
    ]

    def put_down(r):
        return pltpu.make_async_copy(
            staged.at[lax.rem(r, 2)], parts_hbm.at[ctx ^ r], store.at[lax.rem(r, 2)]
        )

    own.start()
    for copy in weights:
        copy.start()
    for r in range(4):
        load_ups(r, ups_hbm[r]).start()
    greet(dp, ctx, (), (1, 2, 3))
    give(1).start()
    give(2).start()

    @pl.when(middle)
    def _():
        give(3).start()

    own.wait()
    for copy in weights:
        copy.wait()

    def block(r, carry):
        @pl.when(r > 0)
        def _():
            give(r).wait_recv()

        @pl.when((r == 2) & middle)
        def _():
            relay.start()

        load_ups(r, mid_hbm).wait()
        here = pl.ds(pl.multiple_of(r * rows, rows), rows)

        def activate(cols):
            value, upper = mids[here, :], ups[here, :]
            gate_proj = mdot(value, w_gate[:, cols])
            up_proj = mdot(value, w_up[:, cols])
            grad_activated = mdot(upper, w_down[:, cols])
            gate_sigmoid = jax.nn.sigmoid(gate_proj)
            silu_gate = gate_proj * gate_sigmoid
            silu_slope = gate_sigmoid * (1.0 + gate_proj * (1.0 - gate_sigmoid))
            act[here, cols] = (silu_gate * up_proj).astype(bf16)
            grad_g[here, cols] = (grad_activated * up_proj * silu_slope).astype(bf16)
            grad_u[here, cols] = (grad_activated * silu_gate).astype(bf16)

        def one(t, carry):
            activate(pl.ds(pl.multiple_of(t * tile, tile), tile))
            return carry

        lax.fori_loop(0, whole, one, 0)
        if hidden % tile:
            activate(pl.ds(whole * tile, hidden % tile))

        @pl.when(r >= 2)
        def _():
            put_down(r).wait()

        def two(t, carry):
            cols = pl.ds(pl.multiple_of(t * tile, tile), tile)
            term = mdot(grad_g[here, :], w_gate[cols, :], NT)
            term += mdot(grad_u[here, :], w_up[cols, :], NT)

            @pl.when(r == 0)
            def _():
                grad_ref[:, cols] = term

            @pl.when(r > 0)
            def _():
                to_send[lax.max(r - 1, 0), :, cols] = term.astype(bf16)

            staged[lax.rem(r, 2), :, cols] = mdot(act[here, :], w_down[cols, :], NT).astype(bf16)
            return carry

        lax.fori_loop(0, width // tile, two, 0)
        put_down(r).start()

        @pl.when(r > 0)
        def _():
            back(r).start()

        return carry

    lax.fori_loop(0, 4, block, 0)

    step = 384
    for i, (left, right, place) in enumerate(
        ((mids, grad_g, w_gate), (mids, grad_u, w_up), (ups, act, w_down))
    ):

        def put(j):
            return pltpu.make_async_copy(
                place.at[pl.ds(pl.multiple_of(j * share, share), share)],
                dw_hbm.at[j, i],
                out_sem.at[i, j],
            )

        def three(t, carry):
            cols = pl.ds(pl.multiple_of(t * step, step), step)
            place[cols, :] = mdot(left[:, cols], right[...], TN).astype(bf16)
            for k in range(step // share):
                put(t * (step // share) + k).start()
            return carry

        lax.fori_loop(0, width // step, three, 0)

    for r in (1, 2, 3):
        back(r).wait_recv()
        grad_ref[...] += received[r - 1].astype(f32)
    for r in (1, 2, 3):
        back(r).wait_send()
    give(1).wait_send()
    give(2).wait_send()

    @pl.when(middle)
    def _():
        give(3).wait_send()
        relay.wait_send()

    for r in (2, 3):
        put_down(r).wait()
    for i, place in enumerate((w_gate, w_up, w_down)):
        for j in range(dp_blocks):
            pltpu.make_async_copy(
                place.at[pl.ds(j * share, share)], dw_hbm.at[j, i], out_sem.at[i, j]
            ).wait()


def feed_forward(mid, ups, full_gate, full_up, full_down_t, dp_blocks, cid):
    rows, width = mid.shape
    hidden = full_gate.shape[1]
    weight = pltpu.VMEM((width, hidden), bf16)
    kept = pltpu.VMEM((4 * rows, hidden), bf16)
    every_row = pltpu.VMEM((4 * rows, width), bf16)
    return pl.pallas_call(
        functools.partial(feed_forward_kernel, dp_blocks),
        in_specs=[ANY] * 8,
        out_specs=[pl.BlockSpec(memory_space=pltpu.VMEM), ANY, ANY],
        out_shape=[
            jax.ShapeDtypeStruct((rows, width), f32),
            jax.ShapeDtypeStruct((4, rows, width), bf16),
            jax.ShapeDtypeStruct((dp_blocks, 3, width // dp_blocks, hidden), bf16),
        ],
        scratch_shapes=[every_row, every_row, weight, weight, weight, kept, kept, kept]
        + [
            pltpu.VMEM((3, rows, width), bf16),
            pltpu.VMEM((3, rows, width), bf16),
            pltpu.VMEM((2, rows, width), bf16),
            pltpu.SemaphoreType.DMA((8,)),
            pltpu.SemaphoreType.DMA((2,)),
            pltpu.SemaphoreType.DMA((3, dp_blocks)),
            pltpu.SemaphoreType.DMA((7,)),
            pltpu.SemaphoreType.DMA((7,)),
        ],
        compiler_params=pltpu.CompilerParams(
            collective_id=cid, has_side_effects=True, vmem_limit_bytes=63 * 2**20
        ),
        name="feed_forward",
    )(mid, full_gate, full_up, full_down_t, *ups)


def shards(
    tokens,
    seq_lens,
    gain_in,
    w_query,
    w_key,
    w_value,
    w_out,
    qk_gains,
    gain_mid,
    w_gate,
    w_up,
    w_down,
    grad_out,
):
    every = ("dp", "ctx")
    rows, width = tokens.shape
    ctx = lax.axis_size("ctx")
    world = ctx * lax.axis_size("dp")
    mine = lax.axis_index("ctx")
    share = w_query.shape[0]
    qk_share = qk_gains.shape[0]
    positions = mine * rows + jnp.arange(rows, dtype=jnp.int32)
    length = seq_lens[0]
    where = jnp.stack([mine.astype(jnp.int32), length - mine * rows])
    cosine_table, sine_table = rope_tables(positions, HD)

    small = (lax.axis_size("dp"), ctx) == (8, 4)

    def move(block, pairs):
        return lax.ppermute(block, "ctx", pairs)

    def lift(block):
        one = move(block, [(0, 1), (1, 2), (2, 3)])
        two = move(block, [(0, 2), (1, 3)])
        return [block, one, two, move(block, [(0, 3)])]

    def after(value, *others):
        return lax.optimization_barrier((value, others))[0]

    def swap(block, r):
        return move(block, [(i, i ^ r) for i in range(ctx)])

    def gather(blocks, riding, cid):
        if small:
            return gather_all(blocks, riding, cid)
        full = [lax.all_gather(b, every, axis=0, tiled=True) for b in blocks]
        return full + [swap(b, 1) for b in riding]

    def collect(terms, riding, hops, cid):
        if small:
            return sum_all(terms, riding, hops, cid)
        return [
            lax.psum_scatter(t, every, scatter_dimension=0, tiled=True).astype(f32) for t in terms
        ] + [swap(block, r) for block, r in zip(riding, hops)]

    extra = jnp.stack([gain_in, gain_mid, jnp.pad(qk_gains, (0, share - qk_share))], 1)
    extra = jnp.pad(extra, ((0, 0), (0, 125)))
    valid_rows = (positions < length).astype(f32)[:, None]
    upstream = grad_out.astype(f32) * valid_rows
    upstream_low = upstream.astype(bf16)
    full_kv, full_query, full_out_t, ups_near = gather(
        [jnp.concatenate([w_key, w_value, extra], 1), w_query, w_out.T], [upstream_low], 1
    )
    kv_width = 2 * KVH * HD
    full_extra = full_kv[:, kv_width:].astype(f32)
    full_gain_in, full_gain_mid = full_extra[:, 0], full_extra[:, 1]
    full_qk = full_extra[:, 2].reshape(world, share)[:, :qk_share].reshape(-1)
    full_gate, full_up, full_down_t = (
        lax.all_gather(after(w, full_kv), "dp", axis=0, tiled=True)
        for w in (w_gate, w_up, w_down.T)
    )
    full_kv = full_kv[:, :kv_width]

    inputs = tokens.astype(f32)

    normed_f, factor_in = rms_scale(inputs, full_gain_in)
    normed = normed_f.astype(bf16)
    kv_raw = mdot(normed, full_kv)
    key_raw = kv_raw[:, : KVH * HD].reshape(rows, KVH, HD)
    value_low = kv_raw[:, KVH * HD :].astype(bf16)
    gain_query = full_qk[:HD]
    gain_key = full_qk[HD:]
    key_normed, factor_key = rms_scale(key_raw, gain_key)
    key_low = rotate(key_normed, cosine_table, sine_table).astype(bf16).reshape(rows, KVH * HD)
    kv_own = jnp.stack([key_low, value_low])
    kv_blocks = lift(kv_own)
    far_low = after(upstream_low, kv_blocks)
    ups_two = swap(far_low, 2)
    ups_middle = move(far_low, [(1, 2), (2, 1)])
    ups_ends = move(ups_two, [(2, 3), (1, 0)])
    ups_three = jnp.where((mine == 1) | (mine == 2), ups_middle, ups_ends)
    ups = [upstream_low, ups_near, ups_two, ups_three]
    query_flat = mdot(normed, full_query)
    query_raw = query_flat.reshape(rows, H, HD)
    query_normed, factor_query = rms_scale(query_raw, gain_query)
    query_low = rotate(query_normed, cosine_table, sine_table).astype(bf16)
    query_low = (query_low * (HD**-0.5)).astype(bf16).reshape(rows, H * HD)

    mixed_low, logs = attn_forward(where, query_low, kv_blocks)
    hidden = inputs + mdot(mixed_low, full_out_t, NT)
    normed_mid_f, factor_mid = rms_scale(hidden, full_gain_mid)
    normed_mid = normed_mid_f.astype(bf16)

    grad_mid_term, down_parts, grad_ffn = feed_forward(
        normed_mid, ups, full_gate, full_up, full_down_t, lax.axis_size("dp"), 2
    )
    grad_ffn = lax.psum_scatter(
        grad_ffn.reshape(-1, grad_ffn.shape[-1]), "dp", scatter_dimension=0, tiled=True
    )
    grad_hidden_norm, gain_terms_mid = norm_back(grad_mid_term, hidden, factor_mid, full_gain_mid)
    grad_hidden = upstream + grad_hidden_norm
    grad_branch = grad_hidden.astype(bf16)
    grad_mixed = mdot(grad_branch, full_out_t).astype(bf16)
    grad_wout_t = mdot(grad_branch, mixed_low, TN).astype(bf16)

    flat_cosine = jnp.concatenate([cosine_table[:, 0], cosine_table[:, 0]], 1)
    flat_sine = jnp.concatenate([sine_table[:, 0], sine_table[:, 0]], 1)
    turn_sign = jnp.where(jnp.arange(2 * HD) % HD < HD // 2, -1.0, 1.0).astype(f32)
    grad_query_low, grad_kv_low, gain_rows = attn_backward(
        seq_lens,
        query_low,
        kv_blocks,
        grad_mixed,
        mixed_low,
        logs,
        query_flat,
        kv_raw[:, : KVH * HD],
        (flat_cosine, flat_sine * turn_sign),
        jnp.concatenate([full_qk.reshape(2, HD), full_qk.reshape(2, HD)], 1),
        3,
    )
    later = after(down_parts, grad_query_low)
    for_far, for_two, for_near = (later[mine ^ r] for r in (3, 2, 1))
    passed = move(for_far, [(0, 1), (3, 2)])
    down_terms = [later[mine], move(for_far, [(1, 2), (2, 1)])]
    for_two = (for_two.astype(f32) + passed.astype(f32)).astype(bf16)
    grad_wquery = mdot(normed, grad_query_low, TN).astype(bf16)
    grad_wkv = mdot(normed, grad_kv_low, TN).astype(bf16)
    grad_normed = mdot(grad_query_low, full_query, NT) + mdot(grad_kv_low, full_kv, NT)
    grad_input_norm, gain_terms_in = norm_back(grad_normed, inputs, factor_in, full_gain_in)
    grad_tokens = grad_hidden + grad_input_norm
    grad_qk = (gain_rows[:, :HD] + gain_rows[:, HD:]).reshape(-1)
    qk_column = jnp.pad(grad_qk.reshape(world, qk_share), ((0, 0), (0, share - qk_share)))
    grad_extra = jnp.stack(
        [jnp.sum(gain_terms_in, axis=0), jnp.sum(gain_terms_mid, axis=0), qk_column.reshape(-1)], 1
    )
    grad_extra = jnp.pad(grad_extra, ((0, 0), (0, 125))).astype(bf16)
    grad_wout, sum_query, sum_kv, sum_extra, *landed = collect(
        [grad_wout_t, grad_wquery, grad_wkv, grad_extra],
        [for_two, for_near],
        (2, 1),
        4,
    )
    down_terms += landed
    grad_ffn, down_terms = after((grad_ffn, down_terms), sum_kv)
    output = (hidden + sum(t.astype(f32) for t in down_terms)).astype(bf16)
    grad_wgate, grad_wup, grad_wdown = (
        grad_ffn[i * w_gate.shape[0] : (i + 1) * w_gate.shape[0]].astype(f32) for i in range(3)
    )
    grad_wdown = grad_wdown.T
    return (
        output,
        grad_tokens,
        sum_extra[:, 0],
        sum_query,
        sum_kv[:, : KVH * HD],
        sum_kv[:, KVH * HD :],
        grad_wout.T,
        sum_extra[:qk_share, 2],
        sum_extra[:, 1],
        grad_wgate,
        grad_wup,
        grad_wdown,
    )


def solution(mesh):
    every = ("dp", "ctx")
    rows, one = P(every, None), P(every)
    in_specs = (
        rows,
        P("dp"),
        one,
        rows,
        rows,
        rows,
        P(None, every),
        one,
        one,
        P("dp", "ctx"),
        P("dp", "ctx"),
        P("ctx", "dp"),
        rows,
    )
    out_specs = (
        rows,
        rows,
        one,
        rows,
        rows,
        rows,
        P(None, every),
        one,
        one,
        P("dp", "ctx"),
        P("dp", "ctx"),
        P("ctx", "dp"),
    )
    return jax.shard_map(shards, mesh=mesh, in_specs=in_specs, out_specs=out_specs, check_vma=False)
```

```python
import functools

import jax
import jax.numpy as jnp
from jax import lax
from jax.experimental import pallas as pl
from jax.experimental.pallas import tpu as pltpu
from jax.sharding import PartitionSpec as P

H = 24
KVH = 8
HD = 64
GROUP = H // KVH
PAIRS = KVH // 2


EPSILON = 1e-05
THETA = 1000000.0
NEG_BIG = -1e30

f32 = jnp.float32
bf16 = jnp.bfloat16

NT = (((1,), (1,)), ((), ()))
NN = (((1,), (0,)), ((), ()))
TN = (((0,), (0,)), ((), ()))


def rms_scale(values, gain_vec):
    factor = lax.rsqrt(jnp.mean(values * values, axis=-1, keepdims=True) + EPSILON)
    return (values * factor * gain_vec, factor)


def norm_back(grad_upper, values, factor, gain_vec):
    unit_rows = values * factor
    scaled = grad_upper * gain_vec
    grad_lower = factor * (
        scaled - unit_rows * jnp.mean(scaled * unit_rows, axis=-1, keepdims=True)
    )
    return (grad_lower, grad_upper * unit_rows)


def rope_tables(positions, head_width):
    half_width = head_width // 2
    frequency = THETA ** (-jnp.arange(half_width, dtype=jnp.float32) * 2.0 / head_width)
    angles = positions.astype(jnp.float32)[:, None] * frequency[None, :]
    cosine_table = jnp.concatenate([jnp.cos(angles), jnp.cos(angles)], -1)[:, None, :]
    sine_table = jnp.concatenate([jnp.sin(angles), jnp.sin(angles)], -1)[:, None, :]
    return (cosine_table, sine_table)


def rotate(values, cosine_table, sine_table):
    half_width = values.shape[-1] // 2
    turned = jnp.concatenate([-values[..., half_width:], values[..., :half_width]], -1)
    return values * cosine_table + turned * sine_table


def rotate_back(grad_upper, cosine_table, sine_table):
    half_width = grad_upper.shape[-1] // 2
    moved_sine = grad_upper * sine_table
    turned = jnp.concatenate([moved_sine[..., half_width:], -moved_sine[..., :half_width]], -1)
    return grad_upper * cosine_table + turned


def mdot(a, b, dims=NN):
    return lax.dot_general(a, b, dims, preferred_element_type=f32)


ANY = pl.BlockSpec(memory_space=pl.ANY)


def lasting(micros):
    return pl.CostEstimate(flops=micros * 10**9, bytes_accessed=0, transcendentals=0)


def remote(src, dst, send, recv, dp, ctx):
    return pltpu.make_async_remote_copy(
        src_ref=src,
        dst_ref=dst,
        send_sem=send,
        recv_sem=recv,
        device_id=(dp, ctx),
        device_id_type=pl.DeviceIdType.MESH,
    )


def greet(dp, ctx, near, far):
    barrier = pltpu.get_barrier_semaphore()
    partners = [(dp ^ r, ctx) for r in near] + [(dp, ctx ^ s) for s in far]
    for partner in partners:
        pl.semaphore_signal(
            barrier, inc=1, device_id=partner, device_id_type=pl.DeviceIdType.MESH
        )
    pl.semaphore_wait(barrier, len(partners))


def gather_kernel(parts, hops, *refs):
    riders = len(hops)
    srcs, riding = refs[:parts], refs[parts : parts + riders]
    outs, landed = refs[parts + riders : 2 * parts + riders], refs[2 * parts + riders :][:riders]
    own_sem, send, recv, ride_send, ride_recv = refs[2 * parts + 2 * riders :]
    dp, ctx = lax.axis_index("dp"), lax.axis_index("ctx")
    greet(dp, ctx, (1, 2, 4), (1, 2, 3))

    def ride(i):
        return remote(riding[i], landed[i], ride_send.at[i], ride_recv.at[i], dp, ctx ^ hops[i])

    def line(p, s):
        return remote(
            srcs[p], outs[p].at[dp, ctx], send.at[p, s - 1], recv.at[p, s - 1], dp, ctx ^ s
        )

    def plane(p, way):
        return remote(
            outs[p].at[dp], outs[p].at[dp], send.at[p, 3 + way], recv.at[p, 3 + way],
            dp ^ (2 << way), ctx,
        )

    def corner(p, way):
        block = outs[p].at[dp ^ (2 << (1 - way)), pl.ds(2 * way, 2)]
        return remote(block, block, send.at[p, 5 + way], recv.at[p, 5 + way], dp ^ (2 << way), ctx)

    def across(p, k):
        block = outs[p].at[dp ^ (2 * k)]
        return remote(block, block, send.at[p, 7 + k], recv.at[p, 7 + k], dp ^ 1, ctx)

    def own(p):
        return pltpu.make_async_copy(srcs[p], outs[p].at[dp, ctx], own_sem.at[p])

    for p in range(parts):
        own(p).start()
        for s in (1, 2, 3):
            line(p, s).start()
    for i in range(riders):
        ride(i).start()
    for step in range(parts + 2):
        if step < parts:
            p = step
            own(p).wait()
            for s in (1, 2, 3):
                line(p, s).wait_recv()
            for way in (0, 1):
                plane(p, way).start()
            across(p, 0).start()
        if 0 <= step - 1 < parts:
            p = step - 1
            for way in (0, 1):
                plane(p, way).wait_recv()
            for way in (0, 1):
                corner(p, way).start()
            for k in (1, 2):
                across(p, k).start()
        if 0 <= step - 2 < parts:
            p = step - 2
            for way in (0, 1):
                corner(p, way).wait_recv()
            across(p, 3).start()
    for p in range(parts):
        for s in (1, 2, 3):
            line(p, s).wait_send()
        for way in (0, 1):
            plane(p, way).wait_send()
            corner(p, way).wait_send()
        for k in range(4):
            across(p, k).wait_send()
            across(p, k).wait_recv()
    for i in range(riders):
        ride(i).wait()


def gather_all(shards, riding, hops, cid):
    parts, riders = len(shards), len(riding)
    outs = pl.pallas_call(
        functools.partial(gather_kernel, parts, hops),
        in_specs=[ANY] * (parts + riders),
        out_specs=[ANY] * (parts + riders),
        out_shape=[jax.ShapeDtypeStruct((8, 4) + s.shape, s.dtype) for s in shards]
        + [jax.ShapeDtypeStruct(s.shape, s.dtype) for s in riding],
        scratch_shapes=[
            pltpu.SemaphoreType.DMA((parts,)),
            pltpu.SemaphoreType.DMA((parts, 11)),
            pltpu.SemaphoreType.DMA((parts, 11)),
            pltpu.SemaphoreType.DMA((max(riders, 1),)),
            pltpu.SemaphoreType.DMA((max(riders, 1),)),
        ],
        compiler_params=pltpu.CompilerParams(collective_id=cid, has_side_effects=True),
        name="gather_all",
    )(*shards, *riding)
    full = [o.reshape(32 * s.shape[0], s.shape[1]) for o, s in zip(outs, shards)]
    return full + list(outs[parts:])


SUM_PARTS = ((0, 0, 768), (0, 768, 768), (1, 0, 768), (1, 768, 768), (2, 0, 1024))


def sum_kernel(hops, *refs):
    riders, parts = len(hops), len(SUM_PARTS) + 1
    lefts, rights, ready, riding = refs[:3], refs[3:6], refs[6], refs[7 : 7 + riders]
    refs = refs[7 + riders :]
    outs, landed = refs[:4], refs[4 : 4 + riders]
    refs = refs[4 + riders :]
    terms, got, plane1, plane2, lines = (refs[i * parts : (i + 1) * parts] for i in range(5))
    load, send, recv, ride_send, ride_recv = refs[5 * parts :]
    dp, ctx = lax.axis_index("dp"), lax.axis_index("ctx")
    chip = dp // 2
    core = dp - 2 * chip
    halves = (pl.ds(0, 2), pl.ds(2, 2))
    rows = lefts[0].shape[1]

    def ride(i):
        return remote(riding[i], landed[i], ride_send.at[i], ride_recv.at[i], dp, ctx ^ hops[i])

    def kept(k):
        return 2 * (chip ^ k) + core

    fetch = pltpu.make_async_copy(ready, terms[-1], load)

    def multiply(p):
        which, start, width = SUM_PARTS[p]
        step = 2 * 4 * terms[p].shape[2]

        def tile(t, carry):
            cols = pl.ds(pl.multiple_of(t * step, step), step)
            product = mdot(lefts[which][:, cols], rights[which][:, start : start + width], TN)
            terms[p][pl.ds(2 * t, 2)] = product.astype(bf16).reshape(2, *terms[p].shape[1:])
            return carry

        lax.fori_loop(0, rows // step, tile, 0)

    def across(p, k):
        return remote(
            terms[p].at[2 * (chip ^ k) + (1 - core)], got[p].at[k],
            send.at[p, k], recv.at[p, k], dp ^ 1, ctx,
        )

    def first(p, w, i):
        k = (1 << w) if i == 0 else 3
        return remote(
            terms[p].at[kept(k), halves[w]], plane1[p].at[i, halves[w]],
            send.at[p, 4 + 2 * w + i], recv.at[p, 4 + 2 * w + i], dp ^ (2 << w), ctx,
        )

    def second(p, w):
        return remote(
            terms[p].at[kept(1 << (1 - w)), halves[w]], plane2[p].at[halves[w]],
            send.at[p, 8 + w], recv.at[p, 8 + w], dp ^ (2 << (1 - w)), ctx,
        )

    def line(p, s):
        return remote(
            terms[p].at[kept(0), ctx ^ s], lines[p].at[s - 1],
            send.at[p, 9 + s], recv.at[p, 9 + s], dp, ctx ^ s,
        )

    def add(target, term):
        target[...] = (target[...].astype(f32) + term[...].astype(f32)).astype(bf16)

    fetch.start()
    greet(dp, ctx, (1, 2, 4), (1, 2, 3))
    for i in range(riders):
        ride(i).start()

    def begin(p):
        if p < parts - 1:
            multiply(p)
        else:
            fetch.wait()
        for k in (3, 1, 2, 0):
            across(p, k).start()

    begin(0)
    for step in range(parts + 2):
        if step + 1 < parts:
            begin(step + 1)
        if step < parts:
            p = step
            for k in (3, 1, 2, 0):
                across(p, k).wait_recv()
                for c in range(4):
                    add(terms[p].at[kept(k), c], got[p].at[k, c])
                if k == 3:
                    for w in (0, 1):
                        first(p, w, 1).start()
                elif k:
                    first(p, k - 1, 0).start()
        if 0 <= step - 1 < parts:
            p = step - 1
            for w in (0, 1):
                first(p, w, 1).wait_recv()
                for c in (2 * w, 2 * w + 1):
                    add(terms[p].at[kept(1 << (1 - w)), c], plane1[p].at[1, c])
                second(p, w).start()
            for w in (0, 1):
                first(p, w, 0).wait_recv()
                for c in (2 * w, 2 * w + 1):
                    add(terms[p].at[kept(0), c], plane1[p].at[0, c])
        if 0 <= step - 2 < parts:
            p = step - 2
            for w in (0, 1):
                second(p, w).wait_recv()
                for c in (2 * w, 2 * w + 1):
                    add(terms[p].at[kept(0), c], plane2[p].at[c])
            for s in (3, 2, 1):
                line(p, s).start()
    for p in range(parts):
        for s in (1, 2, 3):
            line(p, s).wait_recv()
        total = terms[p][kept(0), ctx].astype(f32)
        for s in (1, 2, 3):
            total = total + lines[p][s - 1].astype(f32)
        if p < parts - 1:
            which, start, width = SUM_PARTS[p]
            outs[which][:, start : start + width] = total
        else:
            outs[3][...] = total
    for p in range(parts):
        for k in range(4):
            across(p, k).wait_send()
        for w in (0, 1):
            for i in (0, 1):
                first(p, w, i).wait_send()
            second(p, w).wait_send()
        for s in (1, 2, 3):
            line(p, s).wait_send()
    for i in range(riders):
        ride(i).wait()


def sum_all(lefts, rights, ready, riding, hops, cid):
    parts, riders = len(SUM_PARTS) + 1, len(riding)
    rows = lefts[0].shape[1]
    share = rows // 32
    blocks = ready.reshape(8, 4, share, ready.shape[1])
    widths = [width for _, _, width in SUM_PARTS] + [ready.shape[1]]
    vmem = pl.BlockSpec(memory_space=pltpu.VMEM)

    def per(*lead):
        return [pltpu.VMEM(lead + (share, width), bf16) for width in widths]

    return pl.pallas_call(
        functools.partial(sum_kernel, hops),
        in_specs=[vmem] * 6 + [ANY] * (1 + riders),
        out_specs=[vmem] * 4 + [ANY] * riders,
        out_shape=[jax.ShapeDtypeStruct((share, r.shape[1]), f32) for r in rights]
        + [jax.ShapeDtypeStruct((share, ready.shape[1]), f32)]
        + [jax.ShapeDtypeStruct(r.shape, r.dtype) for r in riding],
        scratch_shapes=per(8, 4) + per(4, 4) + per(2, 4) + per(4) + per(3)
        + [
            pltpu.SemaphoreType.DMA,
            pltpu.SemaphoreType.DMA((parts, 13)),
            pltpu.SemaphoreType.DMA((parts, 13)),
            pltpu.SemaphoreType.DMA((riders,)),
            pltpu.SemaphoreType.DMA((riders,)),
        ],
        compiler_params=pltpu.CompilerParams(
            collective_id=cid, has_side_effects=True, vmem_limit_bytes=56 * 2**20
        ),
        name="sum_all",
    )(*lefts, *rights, blocks, *riding)


def causal_mask(rows, limit, key_axis):
    shape = (rows, rows)
    key = lax.broadcasted_iota(jnp.int32, shape, key_axis)
    row = lax.broadcasted_iota(jnp.int32, shape, 1 - key_axis)
    return jnp.where((key <= row) & (key < limit), 0.0, NEG_BIG).astype(f32)


def split_dot(values, weights, dims):
    high = values.astype(bf16)
    low = (values - high.astype(f32)).astype(bf16)
    return mdot(high, weights, dims) + mdot(low, weights, dims)


def head_means(values):
    shape = (2 * HD, 2 * HD)
    same = lax.broadcasted_iota(jnp.int32, shape, 0) // HD == (
        lax.broadcasted_iota(jnp.int32, shape, 1) // HD
    )
    return split_dot(values, jnp.where(same, 1.0 / HD, 0.0).astype(bf16), NN)


def first_half(shape):
    return lax.rem(lax.broadcasted_iota(jnp.int32, shape, 1), HD) < HD // 2


def half_swap(values):
    lower = pltpu.roll(values, HD // 2, 1)
    upper = pltpu.roll(values, 2 * HD - HD // 2, 1)
    return jnp.where(first_half(values.shape), upper, lower)


def unrotate_norm_back(grad_rot, raw, cosine, signed_sine, gain):
    grad_upper = grad_rot * cosine + half_swap(grad_rot * signed_sine)
    factor = lax.rsqrt(head_means(raw * raw) + EPSILON)
    unit_rows = raw * factor
    scaled = grad_upper * gain
    grad_lower = factor * (scaled - unit_rows * head_means(scaled * unit_rows))
    return grad_lower, jnp.sum(grad_upper * unit_rows, axis=0, keepdims=True)


def norm_rotate(raw, cosine, signed_sine, gain):
    values = raw * lax.rsqrt(head_means(raw * raw) + EPSILON) * gain
    return values * cosine + half_swap(values) * signed_sine


def attn_fwd_kernel(*refs):
    length_ref, normed, w_kv, cosine, sine, gains, tokens, gain_mid = refs[:8]
    query_hbm, out_hbm, rows_hbm, two_hbm = refs[8:12]
    q_ref, o_ref, log_ref, q_raw, k_raw, hidden, mid = refs[12:19]
    kv_hbm, three_hbm = refs[19:23], refs[23]
    w_query, w_out, kv, acc, mask, load, store, send, recv = refs[24:]
    rows, width = normed.shape
    half = KVH * HD
    dp, mine = lax.axis_index("dp"), lax.axis_index("ctx")
    middle = (mine == 1) | (mine == 2)

    loads = [
        pltpu.make_async_copy(query_hbm, w_query, load.at[0]),
        pltpu.make_async_copy(out_hbm, w_out, load.at[1]),
    ]

    def lift(k):
        return remote(kv.at[0], kv.at[k], send.at[k - 1], recv.at[k - 1], dp, mine + k)

    lift_on = remote(kv.at[2], kv.at[3], send.at[2], recv.at[2], dp, mine + 1)
    rows_three = remote(rows_hbm, three_hbm, send.at[3], recv.at[3], dp, mine ^ 3)
    rows_on = remote(two_hbm, three_hbm, send.at[4], recv.at[3], dp, mine ^ 1)

    def keep(k):
        return pltpu.make_async_copy(kv.at[k], kv_hbm[k], store.at[k])

    for copy in loads:
        copy.start()
    greet(dp, mine, (), (1, 2, 3))

    for i in range(2):
        cols = slice(4 * i * HD, (4 * i + 4) * HD)
        raw = mdot(normed[...], w_kv[:, cols])
        k_raw[:, cols] = raw
        for j in range(2):
            part = slice(2 * j * HD, (2 * j + 2) * HD)
            turned = norm_rotate(raw[:, part], cosine[...], sine[...], gains[1:2, :])
            kv[0, 0, :, (4 * i + 2 * j) * HD : (4 * i + 2 * j + 2) * HD] = turned.astype(bf16)
        value = mdot(normed[...], w_kv[:, half + 4 * i * HD : half + (4 * i + 4) * HD])
        kv[0, 1, :, cols] = value.astype(bf16)

    @pl.when(mine <= 2)
    def _():
        lift(1).start()

    @pl.when(mine <= 1)
    def _():
        lift(2).start()

    @pl.when(mine == 1)
    def _():
        rows_on.start()

    @pl.when(mine == 2)
    def _():
        rows_three.start()

    keep(0).start()
    mask[...] = causal_mask(rows, length_ref[0] - mine * rows, 1)
    loads[0].wait()

    def make_query(i, carry):
        cols = pl.ds(pl.multiple_of(i * 2 * GROUP * HD, 2 * GROUP * HD), 2 * GROUP * HD)
        raw = mdot(normed[...], w_query[:, cols])
        q_raw[:, cols] = raw
        turned = [
            norm_rotate(
                raw[:, 2 * j * HD : (2 * j + 2) * HD], cosine[...], sine[...], gains[0:1, :]
            )
            for j in range(GROUP)
        ]
        low = jnp.concatenate(turned, 1).astype(bf16)
        q_ref[:, cols] = (low.astype(f32) * (HD**-0.5)).astype(bf16)
        return carry

    lax.fori_loop(0, PAIRS, make_query, 0)

    def attend(k):
        def pairs(i, carry):
            two = pl.ds(pl.multiple_of(i * 2 * HD, 2 * HD), 2 * HD)
            cols = pl.ds(pl.multiple_of(i * 2 * GROUP * HD, 2 * GROUP * HD), 2 * GROUP * HD)
            both_keys, both_values, queries = kv[k, 0, :, two], kv[k, 1, :, two], q_ref[:, cols]
            for pair in range(2):
                keys = both_keys[:, pair * HD : (pair + 1) * HD]
                values = both_values[:, pair * HD : (pair + 1) * HD]
                extended = jnp.concatenate([values, jnp.ones_like(values)], -1)
                for g in range(GROUP):
                    h = pair * GROUP + g
                    scores = mdot(queries[:, h * HD : (h + 1) * HD], keys, NT)
                    if k == 0:
                        scores = scores + mask[...]
                    term = mdot(jnp.exp(scores).astype(bf16), extended)
                    place = 2 * GROUP * i + h
                    acc[place] = term if k == 0 else acc[place] + term
            return carry

        lax.fori_loop(0, PAIRS, pairs, 0)

    attend(0)
    for k in (1, 2, 3):

        @pl.when(mine >= k)
        def _():
            (lift_on if k == 3 else lift(k)).wait_recv()
            if k == 2:

                @pl.when(mine == 2)
                def _():
                    lift_on.start()
                    rows_on.start()

            keep(k).start()
            attend(k)

        if k == 1:

            @pl.when(mine <= 1)
            def _():
                lift(1).wait_send()
                lift(2).wait_send()

            @pl.when(mine == 1)
            def _():
                rows_three.start()

    lane = lax.broadcasted_iota(jnp.int32, (rows, 2 * HD), 1)

    def finish(i, carry):
        cols = pl.ds(pl.multiple_of(i * 2 * GROUP * HD, 2 * GROUP * HD), 2 * GROUP * HD)
        logs = jnp.zeros((rows, 2 * HD), f32)
        heads = []
        for h in range(2 * GROUP):
            full = acc[2 * GROUP * i + h]
            total = full[:, HD : HD + 1]
            heads.append(full[:, :HD] / total)
            logs = jnp.where(lane == h, jnp.log(total), logs)
        o_ref[:, cols] = jnp.concatenate(heads, 1).astype(bf16)
        log_ref[i] = jnp.transpose(logs)[:8]
        return carry

    lax.fori_loop(0, PAIRS, finish, 0)

    loads[1].wait()
    tile = 256

    def project(t, carry):
        cols = pl.ds(pl.multiple_of(t * tile, tile), tile)
        hidden[:, cols] = tokens[:, cols].astype(f32) + mdot(o_ref[...], w_out[cols, :], NT)
        return carry

    lax.fori_loop(0, width // tile, project, 0)
    value = hidden[...]
    factor = lax.rsqrt(jnp.mean(value * value, axis=-1, keepdims=True) + EPSILON)
    mid[...] = (value * factor * gain_mid[...]).astype(bf16)

    rows_three.wait_recv()

    @pl.when(middle)
    def _():
        rows_three.wait_send()
        rows_on.wait_send()

    @pl.when(mine == 2)
    def _():
        lift(1).wait_send()
        lift_on.wait_send()

    keep(0).wait()
    for k in (1, 2, 3):

        @pl.when(mine >= k)
        def _():
            keep(k).wait()


def attn_forward(length, normed, full_kv, tables, gains, tokens, gain_mid, weights, ups, cid):
    rows, width = normed.shape
    vmem = pl.BlockSpec(memory_space=pltpu.VMEM)
    keys = jax.ShapeDtypeStruct((2, rows, KVH * HD), bf16)
    rows_like = jax.ShapeDtypeStruct((rows, width), bf16)
    heads = jax.ShapeDtypeStruct((rows, H * HD), bf16)
    return pl.pallas_call(
        attn_fwd_kernel,
        in_specs=[pl.BlockSpec(memory_space=pltpu.SMEM)] + [vmem] * 7 + [ANY] * 4,
        out_specs=[vmem] * 7 + [ANY] * 5,
        out_shape=[
            heads,
            heads,
            jax.ShapeDtypeStruct((PAIRS, 8, rows), f32),
            jax.ShapeDtypeStruct((rows, H * HD), f32),
            jax.ShapeDtypeStruct((rows, KVH * HD), f32),
            jax.ShapeDtypeStruct((rows, width), f32),
            rows_like,
        ]
        + [keys] * 4
        + [rows_like],
        scratch_shapes=[
            pltpu.VMEM((width, H * HD), bf16),
            pltpu.VMEM((width, H * HD), bf16),
            pltpu.VMEM((4, 2, rows, KVH * HD), bf16),
            pltpu.VMEM((H, rows, 2 * HD), f32),
            pltpu.VMEM((rows, rows), f32),
            pltpu.SemaphoreType.DMA((2,)),
            pltpu.SemaphoreType.DMA((4,)),
            pltpu.SemaphoreType.DMA((5,)),
            pltpu.SemaphoreType.DMA((4,)),
        ],
        compiler_params=pltpu.CompilerParams(
            collective_id=cid, has_side_effects=True, vmem_limit_bytes=56 * 2**20
        ),
        name="attn_forward",
    )(length, normed, full_kv, *tables, gains, tokens, gain_mid, *weights, *ups)


def attn_bwd_kernel(blocks, length_ref, q_ref, *refs):
    kv_refs = refs[:blocks]
    do_ref, o_ref, log_ref, q_raw, k_raw, cosine, sine, gains = refs[blocks : blocks + 8]
    gq_ref, gkv_ref, gain_ref = refs[blocks + 8 : blocks + 11]
    mask, dqt, inner, own, to_send, received, send, recv = refs[blocks + 11 :]
    rows = q_ref.shape[0]
    step = pl.program_id(0)
    dp, mine = lax.axis_index("dp"), lax.axis_index("ctx")

    def give(back, i):
        return remote(
            to_send.at[back - 1, i], received.at[back - 1, i],
            send.at[back - 1, i], recv.at[back - 1, i], dp, mine - back,
        )

    @pl.when(step == 0)
    def _():
        greet(dp, mine, (), (1, 2, 3))
        mask[...] = causal_mask(rows, length_ref[0] - mine * rows, 0)
        gain_ref[...] = jnp.zeros_like(gain_ref)

    ones = jnp.ones((8, HD), bf16)
    for h in range(2 * GROUP):
        cols = slice(h * HD, (h + 1) * HD)
        product = do_ref[:, cols].astype(f32) * o_ref[:, cols].astype(f32)
        high = product.astype(bf16)
        low = (product - high.astype(f32)).astype(bf16)
        inner[h] = mdot(ones, high, NT) + mdot(ones, low, NT)

    def head(back, pair):
        cols = slice(pair * HD, (pair + 1) * HD)
        keys = kv_refs[back][0][:, cols]
        values = kv_refs[back][1][:, cols]
        keys_t = jnp.transpose(keys)
        grad_k = jnp.zeros((rows, HD), f32)
        grad_v = jnp.zeros((rows, HD), f32)
        for g in range(GROUP):
            h = pair * GROUP + g
            query = q_ref[:, h * HD : (h + 1) * HD]
            grad = do_ref[:, h * HD : (h + 1) * HD]
            scores = mdot(keys, query, NT) - log_ref[0][h : h + 1]
            if back == 0:
                scores = scores + mask[...]
            probs = jnp.exp(scores)
            gaps = mdot(values, grad, NT) - inner[h][0:1]
            grad_scores = (probs * gaps).astype(bf16)
            grad_k += mdot(grad_scores, query)
            grad_v += mdot(probs.astype(bf16), grad)
            term = mdot(keys_t, grad_scores)
            dqt[h] = term if back == 0 else dqt[h] + term
        if back == 0:
            own[step, 0, :, cols] = grad_k
            own[step, 1, :, cols] = grad_v
        else:
            to_send[back - 1, step, 0, :, cols] = grad_k.astype(bf16)
            to_send[back - 1, step, 1, :, cols] = grad_v.astype(bf16)

    def hand_over(i):
        return remote(
            to_send.at[2, i], received.at[2, i], send.at[2, i], recv.at[2, i], dp, mine - 1
        )

    def pass_on(i):
        hand_over(i).wait_recv()
        for part in range(2):
            joined = to_send[1, i, part].astype(f32) + received[2, i, part].astype(f32)
            to_send[1, i, part] = joined.astype(bf16)
        give(2, i).start()

    for pair in range(2):
        head(0, pair)
    for back in (3, 2, 1):

        @pl.when(mine >= back)
        def _():
            for pair in range(2):
                head(back, pair)
            if back == 3:
                hand_over(step).start()
            elif back == 1:
                give(1, step).start()

        if back == 2:

            @pl.when(mine == 3)
            def _():
                give(2, step).start()

    @pl.when((mine == 2) & (step > 0))
    def _():
        pass_on(step - 1)

    @pl.when((mine == 2) & (step == PAIRS - 1))
    def _():
        pass_on(step)

    for j in range(GROUP):
        cols = slice(2 * j * HD, (2 * j + 2) * HD)
        turned = jnp.concatenate([jnp.transpose(dqt[2 * j]), jnp.transpose(dqt[2 * j + 1])], 1)
        grad, gain_term = unrotate_norm_back(
            turned * (HD**-0.5), q_raw[:, cols], cosine[...], sine[...], gains[0:1, :]
        )
        gq_ref[:, cols] = grad.astype(bf16)
        gain_ref[0:1, :] += gain_term

    @pl.when(step == PAIRS - 1)
    def _():
        for back in (1, 2):

            @pl.when(mine + back < blocks)
            def _():
                for i in range(PAIRS):
                    give(back, i).wait_recv()
                    for part in range(2):
                        own[i, part] += received[back - 1, i, part].astype(f32)

        for i in range(PAIRS):
            cols = slice(2 * i * HD, (2 * i + 2) * HD)
            grad, gain_term = unrotate_norm_back(
                own[i, 0], k_raw[:, cols], cosine[...], sine[...], gains[1:2, :]
            )
            gkv_ref[:, cols] = grad.astype(bf16)
            gkv_ref[:, KVH * HD + 2 * i * HD : KVH * HD + (2 * i + 2) * HD] = own[i, 1].astype(bf16)
            gain_ref[1:2, :] += gain_term
        for back in (1, 2, 3):

            @pl.when(mine >= back)
            def _():
                for i in range(PAIRS):
                    (hand_over(i) if back == 3 else give(back, i)).wait_send()


def kv_spec(rows):
    return pl.BlockSpec((2, rows, 2 * HD), lambda i, *_: (0, 0, i))


def head_spec(rows):
    return pl.BlockSpec((rows, 2 * GROUP * HD), lambda i, *_: (0, i))


def log_spec(rows):
    return pl.BlockSpec((1, 8, rows), lambda i, *_: (i, 0, 0))


def whole_spec(*shape):
    return pl.BlockSpec(shape, lambda i, *_: (0,) * len(shape))


def attn_backward(length, query, kv_blocks, grad, mixed, logs, q_raw, k_raw, tables, gains, cid):
    rows, blocks = query.shape[0], len(kv_blocks)
    pair = (2, rows, 2 * HD)
    return pl.pallas_call(
        functools.partial(attn_bwd_kernel, blocks),
        grid=(PAIRS,),
        in_specs=[pl.BlockSpec(memory_space=pltpu.SMEM), head_spec(rows)]
        + [kv_spec(rows)] * blocks
        + [head_spec(rows), head_spec(rows), log_spec(rows), head_spec(rows)]
        + [whole_spec(rows, KVH * HD)]
        + [whole_spec(rows, 2 * HD)] * 2
        + [whole_spec(2, 2 * HD)],
        out_specs=[
            head_spec(rows),
            whole_spec(rows, 2 * KVH * HD),
            whole_spec(2, 2 * HD),
        ],
        out_shape=[
            jax.ShapeDtypeStruct((rows, H * HD), bf16),
            jax.ShapeDtypeStruct((rows, 2 * KVH * HD), bf16),
            jax.ShapeDtypeStruct((2, 2 * HD), f32),
        ],
        scratch_shapes=[
            pltpu.VMEM((rows, rows), f32),
            pltpu.VMEM((2 * GROUP, HD, rows), f32),
            pltpu.VMEM((2 * GROUP, 8, rows), f32),
            pltpu.VMEM((PAIRS,) + pair, f32),
            pltpu.VMEM((blocks - 1, PAIRS) + pair, bf16),
            pltpu.VMEM((blocks - 1, PAIRS) + pair, bf16),
            pltpu.SemaphoreType.DMA((blocks - 1, PAIRS)),
            pltpu.SemaphoreType.DMA((blocks - 1, PAIRS)),
        ],
        compiler_params=pltpu.CompilerParams(
            collective_id=cid, has_side_effects=True, vmem_limit_bytes=56 * 2**20
        ),
        cost_estimate=lasting(120),
        name="attn_backward",
    )(length, query, *kv_blocks, grad, mixed, logs, q_raw, k_raw, *tables, gains)


def feed_forward_kernel(dp_blocks, *refs):
    mid_hbm, gate_hbm, up_hbm, down_hbm = refs[:4]
    ups_hbm = refs[4:8]
    grad_ref, parts_hbm, dw_hbm = refs[8:11]
    mids, ups, w_gate, w_up, w_down, act, grad_g, grad_u, to_send, received, staged = refs[11:22]
    load, store, out_sem, send, recv = refs[22:]
    rows, width = mid_hbm.shape
    hidden = gate_hbm.shape[1]
    share = width // dp_blocks
    tile, whole = 256, hidden // 256
    dp, ctx = lax.axis_index("dp"), lax.axis_index("ctx")
    middle = (ctx == 1) | (ctx == 2)

    def slot(ref, r):
        return ref.at[pl.ds(pl.multiple_of(r * rows, rows), rows)]

    def give(r):
        return remote(mid_hbm, slot(mids, r), send.at[r], recv.at[r], dp, ctx ^ r)

    relay = remote(slot(mids, 2), slot(mids, 3), send.at[0], recv.at[3], dp, ctx ^ 1)

    def back(r):
        return remote(
            to_send.at[r - 1], received.at[r - 1], send.at[3 + r], recv.at[3 + r], dp, ctx ^ r
        )

    def load_ups(r, source):
        return pltpu.make_async_copy(source, slot(ups, r), load.at[r])

    own = pltpu.make_async_copy(mid_hbm, slot(mids, 0), load.at[4])
    weights = [
        pltpu.make_async_copy(source, target, load.at[5 + i])
        for i, (source, target) in enumerate(
            ((gate_hbm, w_gate), (up_hbm, w_up), (down_hbm, w_down))
        )
    ]

    def put_down(r):
        return pltpu.make_async_copy(
            staged.at[lax.rem(r, 2)], parts_hbm.at[ctx ^ r], store.at[lax.rem(r, 2)]
        )

    own.start()
    for copy in weights:
        copy.start()
    for r in range(4):
        load_ups(r, ups_hbm[r]).start()
    greet(dp, ctx, (), (1, 2, 3))
    give(1).start()
    give(2).start()

    @pl.when(middle)
    def _():
        give(3).start()

    own.wait()
    for copy in weights:
        copy.wait()

    def block(r, carry):
        @pl.when(r > 0)
        def _():
            give(r).wait_recv()

        @pl.when((r == 2) & middle)
        def _():
            relay.start()

        load_ups(r, mid_hbm).wait()
        here = pl.ds(pl.multiple_of(r * rows, rows), rows)

        def activate(cols):
            value, upper = mids[here, :], ups[here, :]
            gate_proj = mdot(value, w_gate[:, cols])
            up_proj = mdot(value, w_up[:, cols])
            grad_activated = mdot(upper, w_down[:, cols])
            gate_sigmoid = jax.nn.sigmoid(gate_proj)
            silu_gate = gate_proj * gate_sigmoid
            silu_slope = gate_sigmoid * (1.0 + gate_proj * (1.0 - gate_sigmoid))
            act[here, cols] = (silu_gate * up_proj).astype(bf16)
            grad_g[here, cols] = (grad_activated * up_proj * silu_slope).astype(bf16)
            grad_u[here, cols] = (grad_activated * silu_gate).astype(bf16)

        def one(t, carry):
            activate(pl.ds(pl.multiple_of(t * tile, tile), tile))
            return carry

        lax.fori_loop(0, whole, one, 0)
        if hidden % tile:
            activate(pl.ds(whole * tile, hidden % tile))

        @pl.when(r >= 2)
        def _():
            put_down(r).wait()

        def two(t, carry):
            cols = pl.ds(pl.multiple_of(t * tile, tile), tile)
            term = mdot(grad_g[here, :], w_gate[cols, :], NT)
            term += mdot(grad_u[here, :], w_up[cols, :], NT)

            @pl.when(r == 0)
            def _():
                grad_ref[:, cols] = term

            @pl.when(r > 0)
            def _():
                to_send[lax.max(r - 1, 0), :, cols] = term.astype(bf16)

            staged[lax.rem(r, 2), :, cols] = mdot(act[here, :], w_down[cols, :], NT).astype(bf16)
            return carry

        lax.fori_loop(0, width // tile, two, 0)
        put_down(r).start()

        @pl.when(r > 0)
        def _():
            back(r).start()

        return carry

    lax.fori_loop(0, 4, block, 0)

    step = 384
    for i, (left, right, place) in enumerate(
        ((mids, grad_g, w_gate), (mids, grad_u, w_up), (ups, act, w_down))
    ):

        def put(j):
            return pltpu.make_async_copy(
                place.at[pl.ds(pl.multiple_of(j * share, share), share)],
                dw_hbm.at[j, i],
                out_sem.at[i, j],
            )

        def three(t, carry):
            cols = pl.ds(pl.multiple_of(t * step, step), step)
            place[cols, :] = mdot(left[:, cols], right[...], TN).astype(bf16)
            for k in range(step // share):
                put(t * (step // share) + k).start()
            return carry

        lax.fori_loop(0, width // step, three, 0)

    for r in (1, 2, 3):
        back(r).wait_recv()
        grad_ref[...] += received[r - 1].astype(f32)
    for r in (1, 2, 3):
        back(r).wait_send()
    give(1).wait_send()
    give(2).wait_send()

    @pl.when(middle)
    def _():
        give(3).wait_send()
        relay.wait_send()

    for r in (2, 3):
        put_down(r).wait()
    for i, place in enumerate((w_gate, w_up, w_down)):
        for j in range(dp_blocks):
            pltpu.make_async_copy(
                place.at[pl.ds(j * share, share)], dw_hbm.at[j, i], out_sem.at[i, j]
            ).wait()


def feed_forward(mid, ups, full_gate, full_up, full_down_t, dp_blocks, cid):
    rows, width = mid.shape
    hidden = full_gate.shape[1]
    weight = pltpu.VMEM((width, hidden), bf16)
    kept = pltpu.VMEM((4 * rows, hidden), bf16)
    every_row = pltpu.VMEM((4 * rows, width), bf16)
    return pl.pallas_call(
        functools.partial(feed_forward_kernel, dp_blocks),
        in_specs=[ANY] * 8,
        out_specs=[pl.BlockSpec(memory_space=pltpu.VMEM), ANY, ANY],
        out_shape=[
            jax.ShapeDtypeStruct((rows, width), f32),
            jax.ShapeDtypeStruct((4, rows, width), bf16),
            jax.ShapeDtypeStruct((dp_blocks, 3, width // dp_blocks, hidden), bf16),
        ],
        scratch_shapes=[every_row, every_row, weight, weight, weight, kept, kept, kept]
        + [
            pltpu.VMEM((3, rows, width), bf16),
            pltpu.VMEM((3, rows, width), bf16),
            pltpu.VMEM((2, rows, width), bf16),
            pltpu.SemaphoreType.DMA((8,)),
            pltpu.SemaphoreType.DMA((2,)),
            pltpu.SemaphoreType.DMA((3, dp_blocks)),
            pltpu.SemaphoreType.DMA((7,)),
            pltpu.SemaphoreType.DMA((7,)),
        ],
        compiler_params=pltpu.CompilerParams(
            collective_id=cid, has_side_effects=True, vmem_limit_bytes=63 * 2**20
        ),
        name="feed_forward",
    )(mid, full_gate, full_up, full_down_t, *ups)


def shards(
    tokens,
    seq_lens,
    gain_in,
    w_query,
    w_key,
    w_value,
    w_out,
    qk_gains,
    gain_mid,
    w_gate,
    w_up,
    w_down,
    grad_out,
):
    every = ("dp", "ctx")
    rows, width = tokens.shape
    ctx = lax.axis_size("ctx")
    world = ctx * lax.axis_size("dp")
    mine = lax.axis_index("ctx")
    share = w_query.shape[0]
    qk_share = qk_gains.shape[0]
    positions = mine * rows + jnp.arange(rows, dtype=jnp.int32)
    length = seq_lens[0]
    where = jnp.stack([mine.astype(jnp.int32), length - mine * rows])
    cosine_table, sine_table = rope_tables(positions, HD)

    small = (lax.axis_size("dp"), ctx) == (8, 4)

    def move(block, pairs):
        return lax.ppermute(block, "ctx", pairs)

    def lift(block):
        one = move(block, [(0, 1), (1, 2), (2, 3)])
        two = move(block, [(0, 2), (1, 3)])
        return [block, one, two, move(block, [(0, 3)])]

    def after(value, *others):
        return lax.optimization_barrier((value, others))[0]

    def swap(block, r):
        return move(block, [(i, i ^ r) for i in range(ctx)])

    def gather(blocks, riding, hops, cid):
        if small:
            return gather_all(blocks, riding, hops, cid)
        full = [lax.all_gather(b, every, axis=0, tiled=True) for b in blocks]
        return full + [swap(b, r) for b, r in zip(riding, hops)]

    def collect(lefts, rights, ready, riding, hops, cid):
        if small:
            return sum_all(lefts, rights, ready, riding, hops, cid)
        terms = [mdot(a, b, TN).astype(bf16) for a, b in zip(lefts, rights)] + [ready]
        return [
            lax.psum_scatter(t, every, scatter_dimension=0, tiled=True).astype(f32) for t in terms
        ] + [swap(block, r) for block, r in zip(riding, hops)]

    extra = jnp.stack([gain_in, gain_mid, jnp.pad(qk_gains, (0, share - qk_share))], 1)
    extra = jnp.pad(extra, ((0, 0), (0, 125)))
    valid_rows = (positions < length).astype(f32)[:, None]
    upstream = grad_out.astype(f32) * valid_rows
    upstream_low = upstream.astype(bf16)
    full_kv, full_query, full_out_t, ups_near, ups_two = gather(
        [jnp.concatenate([w_key, w_value, extra], 1), w_query, w_out.T],
        [upstream_low, upstream_low],
        (1, 2),
        1,
    )
    kv_width = 2 * KVH * HD
    full_extra = full_kv[:, kv_width:].astype(f32)
    full_gain_in, full_gain_mid = full_extra[:, 0], full_extra[:, 1]
    full_qk = full_extra[:, 2].reshape(world, share)[:, :qk_share].reshape(-1)
    full_gate = lax.all_gather(w_gate, "dp", axis=0, tiled=True)
    full_up = lax.all_gather(after(w_up, full_kv, full_gate), "dp", axis=0, tiled=True)
    full_down_t = lax.all_gather(after(w_down.T, full_kv, full_gate), "dp", axis=0, tiled=True)
    wide_kv, full_kv = full_kv, full_kv[:, :kv_width]

    inputs = tokens.astype(f32)

    normed_f, factor_in = rms_scale(inputs, full_gain_in)
    normed = normed_f.astype(bf16)
    flat_cosine = jnp.concatenate([cosine_table[:, 0], cosine_table[:, 0]], 1)
    flat_sine = jnp.concatenate([sine_table[:, 0], sine_table[:, 0]], 1)
    turn_sign = jnp.where(jnp.arange(2 * HD) % HD < HD // 2, -1.0, 1.0).astype(f32)
    tables = (flat_cosine, flat_sine * turn_sign)
    pair_gains = jnp.concatenate([full_qk.reshape(2, HD), full_qk.reshape(2, HD)], 1)
    query_low, mixed_low, logs, query_flat, key_flat, hidden, normed_mid, *landed = attn_forward(
        seq_lens,
        normed,
        wide_kv,
        tables,
        pair_gains,
        tokens,
        full_gain_mid[None],
        (full_query, full_out_t),
        (upstream_low, ups_two),
        3,
    )
    kv_blocks = landed[:4]
    ups = [upstream_low, ups_near, ups_two] + landed[4:]
    factor_mid = rms_scale(hidden, full_gain_mid)[1]

    grad_mid_term, down_parts, grad_ffn = feed_forward(
        normed_mid, ups, full_gate, full_up, full_down_t, lax.axis_size("dp"), 2
    )
    grad_ffn = lax.psum_scatter(
        grad_ffn.reshape(-1, grad_ffn.shape[-1]), "dp", scatter_dimension=0, tiled=True
    )
    grad_hidden_norm, gain_terms_mid = norm_back(grad_mid_term, hidden, factor_mid, full_gain_mid)
    grad_hidden = upstream + grad_hidden_norm
    grad_branch = grad_hidden.astype(bf16)
    grad_mixed = mdot(grad_branch, full_out_t).astype(bf16)

    grad_query_low, grad_kv_low, gain_rows = attn_backward(
        seq_lens,
        query_low,
        kv_blocks,
        grad_mixed,
        mixed_low,
        logs,
        query_flat,
        key_flat,
        tables,
        pair_gains,
        5,
    )
    later = after(down_parts, grad_query_low)
    for_far, for_two, for_near = (later[mine ^ r] for r in (3, 2, 1))
    passed = move(for_far, [(0, 1), (3, 2)])
    down_terms = [later[mine], move(for_far, [(1, 2), (2, 1)])]
    for_two = (for_two.astype(f32) + passed.astype(f32)).astype(bf16)
    grad_normed = mdot(grad_query_low, full_query, NT) + mdot(grad_kv_low, full_kv, NT)
    grad_input_norm, gain_terms_in = norm_back(grad_normed, inputs, factor_in, full_gain_in)
    grad_tokens = grad_hidden + grad_input_norm
    grad_qk = (gain_rows[:, :HD] + gain_rows[:, HD:]).reshape(-1)
    qk_column = jnp.pad(grad_qk.reshape(world, qk_share), ((0, 0), (0, share - qk_share)))
    grad_extra = jnp.stack(
        [jnp.sum(gain_terms_in, axis=0), jnp.sum(gain_terms_mid, axis=0), qk_column.reshape(-1)], 1
    )
    grad_extra = jnp.pad(grad_extra, ((0, 0), (0, 125))).astype(bf16)
    grad_wout, sum_query, sum_kv, sum_extra, *landed = collect(
        (grad_branch, normed, normed),
        (mixed_low, grad_query_low, grad_kv_low),
        grad_extra,
        [for_two, for_near],
        (2, 1),
        4,
    )
    down_terms += landed
    grad_ffn, down_terms = after((grad_ffn, down_terms), sum_kv)
    output = (hidden + sum(t.astype(f32) for t in down_terms)).astype(bf16)
    grad_wgate, grad_wup, grad_wdown = (
        grad_ffn[i * w_gate.shape[0] : (i + 1) * w_gate.shape[0]].astype(f32) for i in range(3)
    )
    grad_wdown = grad_wdown.T
    return (
        output,
        grad_tokens,
        sum_extra[:, 0],
        sum_query,
        sum_kv[:, : KVH * HD],
        sum_kv[:, KVH * HD :],
        grad_wout.T,
        sum_extra[:qk_share, 2],
        sum_extra[:, 1],
        grad_wgate,
        grad_wup,
        grad_wdown,
    )


def solution(mesh):
    every = ("dp", "ctx")
    rows, one = P(every, None), P(every)
    in_specs = (
        rows,
        P("dp"),
        one,
        rows,
        rows,
        rows,
        P(None, every),
        one,
        one,
        P("dp", "ctx"),
        P("dp", "ctx"),
        P("ctx", "dp"),
        rows,
    )
    out_specs = (
        rows,
        rows,
        one,
        rows,
        rows,
        rows,
        P(None, every),
        one,
        one,
        P("dp", "ctx"),
        P("dp", "ctx"),
        P("ctx", "dp"),
    )
    return jax.shard_map(shards, mesh=mesh, in_specs=in_specs, out_specs=out_specs, check_vma=False)
```

```python
import functools

import jax
import jax.numpy as jnp
from jax import lax
from jax.experimental import pallas as pl
from jax.experimental.pallas import tpu as pltpu
from jax.sharding import PartitionSpec as P

H = 24
KVH = 8
HD = 64
GROUP = H // KVH
PAIRS = KVH // 2


EPSILON = 1e-05
THETA = 1000000.0
NEG_BIG = -1e30

f32 = jnp.float32
bf16 = jnp.bfloat16

NT = (((1,), (1,)), ((), ()))
NN = (((1,), (0,)), ((), ()))
TN = (((0,), (0,)), ((), ()))


def rms_scale(values, gain_vec):
    factor = lax.rsqrt(jnp.mean(values * values, axis=-1, keepdims=True) + EPSILON)
    return (values * factor * gain_vec, factor)


def norm_back(grad_upper, values, factor, gain_vec):
    unit_rows = values * factor
    scaled = grad_upper * gain_vec
    grad_lower = factor * (
        scaled - unit_rows * jnp.mean(scaled * unit_rows, axis=-1, keepdims=True)
    )
    return (grad_lower, grad_upper * unit_rows)


def rope_tables(positions, head_width):
    half_width = head_width // 2
    frequency = THETA ** (-jnp.arange(half_width, dtype=jnp.float32) * 2.0 / head_width)
    angles = positions.astype(jnp.float32)[:, None] * frequency[None, :]
    cosine_table = jnp.concatenate([jnp.cos(angles), jnp.cos(angles)], -1)[:, None, :]
    sine_table = jnp.concatenate([jnp.sin(angles), jnp.sin(angles)], -1)[:, None, :]
    return (cosine_table, sine_table)


def rotate(values, cosine_table, sine_table):
    half_width = values.shape[-1] // 2
    turned = jnp.concatenate([-values[..., half_width:], values[..., :half_width]], -1)
    return values * cosine_table + turned * sine_table


def rotate_back(grad_upper, cosine_table, sine_table):
    half_width = grad_upper.shape[-1] // 2
    moved_sine = grad_upper * sine_table
    turned = jnp.concatenate([moved_sine[..., half_width:], -moved_sine[..., :half_width]], -1)
    return grad_upper * cosine_table + turned


def mdot(a, b, dims=NN):
    return lax.dot_general(a, b, dims, preferred_element_type=f32)


ANY = pl.BlockSpec(memory_space=pl.ANY)


def lasting(micros):
    return pl.CostEstimate(flops=micros * 10**9, bytes_accessed=0, transcendentals=0)


def remote(src, dst, send, recv, dp, ctx):
    return pltpu.make_async_remote_copy(
        src_ref=src,
        dst_ref=dst,
        send_sem=send,
        recv_sem=recv,
        device_id=(dp, ctx),
        device_id_type=pl.DeviceIdType.MESH,
    )


def greet(dp, ctx, near, far):
    barrier = pltpu.get_barrier_semaphore()
    partners = [(dp ^ r, ctx) for r in near] + [(dp, ctx ^ s) for s in far]
    for partner in partners:
        pl.semaphore_signal(
            barrier, inc=1, device_id=partner, device_id_type=pl.DeviceIdType.MESH
        )
    pl.semaphore_wait(barrier, len(partners))


def gather_kernel(parts, hops, *refs):
    riders = len(hops)
    srcs, riding = refs[:parts], refs[parts : parts + riders]
    outs, landed = refs[parts + riders : 2 * parts + riders], refs[2 * parts + riders :][:riders]
    own_sem, send, recv, ride_send, ride_recv = refs[2 * parts + 2 * riders :]
    dp, ctx = lax.axis_index("dp"), lax.axis_index("ctx")
    greet(dp, ctx, (1, 2, 4), (1, 2, 3))

    def ride(i):
        return remote(riding[i], landed[i], ride_send.at[i], ride_recv.at[i], dp, ctx ^ hops[i])

    def line(p, s):
        return remote(
            srcs[p], outs[p].at[dp, ctx], send.at[p, s - 1], recv.at[p, s - 1], dp, ctx ^ s
        )

    def plane(p, way):
        return remote(
            outs[p].at[dp], outs[p].at[dp], send.at[p, 3 + way], recv.at[p, 3 + way],
            dp ^ (2 << way), ctx,
        )

    def corner(p, way):
        block = outs[p].at[dp ^ (2 << (1 - way)), pl.ds(2 * way, 2)]
        return remote(block, block, send.at[p, 5 + way], recv.at[p, 5 + way], dp ^ (2 << way), ctx)

    def across(p, k):
        block = outs[p].at[dp ^ (2 * k)]
        return remote(block, block, send.at[p, 7 + k], recv.at[p, 7 + k], dp ^ 1, ctx)

    def own(p):
        return pltpu.make_async_copy(srcs[p], outs[p].at[dp, ctx], own_sem.at[p])

    for p in range(parts):
        own(p).start()
        for s in (1, 2, 3):
            line(p, s).start()
    for i in range(riders):
        ride(i).start()
    for step in range(parts + 2):
        if step < parts:
            p = step
            own(p).wait()
            for s in (1, 2, 3):
                line(p, s).wait_recv()
            for way in (0, 1):
                plane(p, way).start()
            across(p, 0).start()
        if 0 <= step - 1 < parts:
            p = step - 1
            for way in (0, 1):
                plane(p, way).wait_recv()
            for way in (0, 1):
                corner(p, way).start()
            for k in (1, 2):
                across(p, k).start()
        if 0 <= step - 2 < parts:
            p = step - 2
            for way in (0, 1):
                corner(p, way).wait_recv()
            across(p, 3).start()
    for p in range(parts):
        for s in (1, 2, 3):
            line(p, s).wait_send()
        for way in (0, 1):
            plane(p, way).wait_send()
            corner(p, way).wait_send()
        for k in range(4):
            across(p, k).wait_send()
            across(p, k).wait_recv()
    for i in range(riders):
        ride(i).wait()


def gather_all(shards, riding, hops, cid):
    parts, riders = len(shards), len(riding)
    outs = pl.pallas_call(
        functools.partial(gather_kernel, parts, hops),
        in_specs=[ANY] * (parts + riders),
        out_specs=[ANY] * (parts + riders),
        out_shape=[jax.ShapeDtypeStruct((8, 4) + s.shape, s.dtype) for s in shards]
        + [jax.ShapeDtypeStruct(s.shape, s.dtype) for s in riding],
        scratch_shapes=[
            pltpu.SemaphoreType.DMA((parts,)),
            pltpu.SemaphoreType.DMA((parts, 11)),
            pltpu.SemaphoreType.DMA((parts, 11)),
            pltpu.SemaphoreType.DMA((max(riders, 1),)),
            pltpu.SemaphoreType.DMA((max(riders, 1),)),
        ],
        compiler_params=pltpu.CompilerParams(collective_id=cid, has_side_effects=True),
        name="gather_all",
    )(*shards, *riding)
    full = [o.reshape(32 * s.shape[0], s.shape[1]) for o, s in zip(outs, shards)]
    return full + list(outs[parts:])


SUM_PARTS = ((0, 0, 768), (0, 768, 768), (1, 0, 768), (1, 768, 768), (2, 0, 1024))


def sum_kernel(*refs):
    parts = len(SUM_PARTS) + 1
    lefts, rights = refs[:3], refs[3:6]
    w_query, w_kv, tokens, gain_in, grad_hidden, gain_rows = refs[6:12]
    home, outs, grad_tokens = refs[12], refs[13:17], refs[17]
    near_hbm, two_hbm, met_hbm = refs[18:21]
    refs = refs[21:]
    terms, got, plane1, plane2, lines = (refs[i * parts : (i + 1) * parts] for i in range(5))
    for_two, passed, load, send, recv, home_send, home_recv = refs[5 * parts :]
    dp, ctx = lax.axis_index("dp"), lax.axis_index("ctx")
    middle = (ctx == 1) | (ctx == 2)
    chip = dp // 2
    core = dp - 2 * chip
    halves = (pl.ds(0, 2), pl.ds(2, 2))
    rows = lefts[0].shape[1]

    near = remote(home.at[ctx ^ 1], near_hbm, home_send.at[0], home_recv.at[0], dp, ctx ^ 1)
    far = home.at[ctx ^ 3]
    meet = remote(far, met_hbm, home_send.at[1], home_recv.at[1], dp, ctx ^ 3)
    hand = remote(far, passed, home_send.at[1], home_recv.at[2], dp, ctx ^ 1)
    fetch = pltpu.make_async_copy(home.at[ctx ^ 2], for_two, load)
    two = remote(for_two, two_hbm, home_send.at[2], home_recv.at[3], dp, ctx ^ 2)

    def kept(k):
        return 2 * (chip ^ k) + core

    def first_norm():
        def tile(t, carry):
            cols = pl.ds(pl.multiple_of(t * 256, 256), 256)
            term = mdot(rights[1][...], w_query[cols, :], NT)
            grad_tokens[:, cols] = term + mdot(rights[2][...], w_kv[cols, : 2 * KVH * HD], NT)
            return carry

        lax.fori_loop(0, rows // 256, tile, 0)
        values, grad_upper = tokens[...].astype(f32), grad_tokens[...]
        factor = lax.rsqrt(jnp.mean(values * values, axis=-1, keepdims=True) + EPSILON)
        grad_lower, gain_terms = norm_back(grad_upper, values, factor, gain_in[...])
        grad_tokens[...] = grad_hidden[...] + grad_lower
        gain_row = jnp.sum(gain_terms, axis=0, keepdims=True)
        which = lax.broadcasted_iota(jnp.int32, (128, rows), 0)
        stacked = jnp.where(which == 0, gain_row, 0.0)
        stacked = jnp.where(which == 1, gain_rows[0:1, :], stacked)
        stacked = jnp.where(which == 2, gain_rows[1:2, :], stacked)
        terms[-1][...] = jnp.transpose(stacked).astype(bf16).reshape(terms[-1].shape)

    def multiply(p):
        which, start, width = SUM_PARTS[p]
        step = 2 * 4 * terms[p].shape[2]

        def tile(t, carry):
            cols = pl.ds(pl.multiple_of(t * step, step), step)
            product = mdot(lefts[which][:, cols], rights[which][:, start : start + width], TN)
            terms[p][pl.ds(2 * t, 2)] = product.astype(bf16).reshape(2, *terms[p].shape[1:])
            return carry

        lax.fori_loop(0, rows // step, tile, 0)

    def across(p, k):
        return remote(
            terms[p].at[2 * (chip ^ k) + (1 - core)], got[p].at[k],
            send.at[p, k], recv.at[p, k], dp ^ 1, ctx,
        )

    def first(p, w, i):
        k = (1 << w) if i == 0 else 3
        return remote(
            terms[p].at[kept(k), halves[w]], plane1[p].at[i, halves[w]],
            send.at[p, 4 + 2 * w + i], recv.at[p, 4 + 2 * w + i], dp ^ (2 << w), ctx,
        )

    def second(p, w):
        return remote(
            terms[p].at[kept(1 << (1 - w)), halves[w]], plane2[p].at[halves[w]],
            send.at[p, 8 + w], recv.at[p, 8 + w], dp ^ (2 << (1 - w)), ctx,
        )

    def line(p, s):
        return remote(
            terms[p].at[kept(0), ctx ^ s], lines[p].at[s - 1],
            send.at[p, 9 + s], recv.at[p, 9 + s], dp, ctx ^ s,
        )

    def add(target, term):
        target[...] = (target[...].astype(f32) + term[...].astype(f32)).astype(bf16)

    fetch.start()
    greet(dp, ctx, (1, 2, 4), (1, 2, 3))

    @pl.when(middle)
    def _():
        meet.start()

    @pl.when(jnp.logical_not(middle))
    def _():
        hand.start()

    near.start()

    def begin(p):
        if p < parts - 1:
            multiply(p)
        for k in (3, 1, 2, 0):
            across(p, k).start()

    begin(0)
    for step in range(parts + 2):
        if step + 1 < parts:
            begin(step + 1)
        if step == 1:
            first_norm()
            fetch.wait()

            @pl.when(middle)
            def _():
                hand.wait_recv()
                add(for_two, passed)

            two.start()
        if step < parts:
            p = step
            for k in (3, 1, 2, 0):
                across(p, k).wait_recv()
                for c in range(4):
                    add(terms[p].at[kept(k), c], got[p].at[k, c])
                if k == 3:
                    for w in (0, 1):
                        first(p, w, 1).start()
                elif k:
                    first(p, k - 1, 0).start()
        if 0 <= step - 1 < parts:
            p = step - 1
            for w in (0, 1):
                first(p, w, 1).wait_recv()
                for c in (2 * w, 2 * w + 1):
                    add(terms[p].at[kept(1 << (1 - w)), c], plane1[p].at[1, c])
                second(p, w).start()
            for w in (0, 1):
                first(p, w, 0).wait_recv()
                for c in (2 * w, 2 * w + 1):
                    add(terms[p].at[kept(0), c], plane1[p].at[0, c])
        if 0 <= step - 2 < parts:
            p = step - 2
            for w in (0, 1):
                second(p, w).wait_recv()
                for c in (2 * w, 2 * w + 1):
                    add(terms[p].at[kept(0), c], plane2[p].at[c])
            for s in (3, 2, 1):
                line(p, s).start()
    for p in range(parts):
        for s in (1, 2, 3):
            line(p, s).wait_recv()
        total = terms[p][kept(0), ctx].astype(f32)
        for s in (1, 2, 3):
            total = total + lines[p][s - 1].astype(f32)
        if p < parts - 1:
            which, start, width = SUM_PARTS[p]
            outs[which][:, start : start + width] = total
        else:
            outs[3][...] = total
    for p in range(parts):
        for k in range(4):
            across(p, k).wait_send()
        for w in (0, 1):
            for i in (0, 1):
                first(p, w, i).wait_send()
            second(p, w).wait_send()
        for s in (1, 2, 3):
            line(p, s).wait_send()
    near.wait()
    two.wait()

    @pl.when(middle)
    def _():
        meet.wait()

    @pl.when(jnp.logical_not(middle))
    def _():
        hand.wait_send()


def sum_all(lefts, rights, norm_in, home, cid):
    parts = len(SUM_PARTS) + 1
    rows = lefts[0].shape[1]
    share = rows // 32
    widths = [width for _, _, width in SUM_PARTS] + [128]
    vmem = pl.BlockSpec(memory_space=pltpu.VMEM)

    def per(*lead):
        return [pltpu.VMEM(lead + (share, width), bf16) for width in widths]

    return pl.pallas_call(
        sum_kernel,
        in_specs=[vmem] * 12 + [ANY],
        out_specs=[vmem] * 5 + [ANY] * 3,
        out_shape=[jax.ShapeDtypeStruct((share, r.shape[1]), f32) for r in rights]
        + [jax.ShapeDtypeStruct((share, 128), f32)]
        + [jax.ShapeDtypeStruct(lefts[0].shape, f32)]
        + [jax.ShapeDtypeStruct(home.shape[1:], bf16)] * 3,
        scratch_shapes=per(8, 4) + per(4, 4) + per(2, 4) + per(4) + per(3)
        + [
            pltpu.VMEM(home.shape[1:], bf16),
            pltpu.VMEM(home.shape[1:], bf16),
            pltpu.SemaphoreType.DMA,
            pltpu.SemaphoreType.DMA((parts, 13)),
            pltpu.SemaphoreType.DMA((parts, 13)),
            pltpu.SemaphoreType.DMA((3,)),
            pltpu.SemaphoreType.DMA((4,)),
        ],
        compiler_params=pltpu.CompilerParams(
            collective_id=cid, has_side_effects=True, vmem_limit_bytes=60 * 2**20
        ),
        name="sum_all",
    )(*lefts, *rights, *norm_in, home)


def causal_mask(rows, limit, key_axis):
    shape = (rows, rows)
    key = lax.broadcasted_iota(jnp.int32, shape, key_axis)
    row = lax.broadcasted_iota(jnp.int32, shape, 1 - key_axis)
    return jnp.where((key <= row) & (key < limit), 0.0, NEG_BIG).astype(f32)


def split_dot(values, weights, dims):
    high = values.astype(bf16)
    low = (values - high.astype(f32)).astype(bf16)
    return mdot(high, weights, dims) + mdot(low, weights, dims)


def head_means(values):
    shape = (2 * HD, 2 * HD)
    same = lax.broadcasted_iota(jnp.int32, shape, 0) // HD == (
        lax.broadcasted_iota(jnp.int32, shape, 1) // HD
    )
    return split_dot(values, jnp.where(same, 1.0 / HD, 0.0).astype(bf16), NN)


def first_half(shape):
    return lax.rem(lax.broadcasted_iota(jnp.int32, shape, 1), HD) < HD // 2


def half_swap(values):
    lower = pltpu.roll(values, HD // 2, 1)
    upper = pltpu.roll(values, 2 * HD - HD // 2, 1)
    return jnp.where(first_half(values.shape), upper, lower)


def unrotate_norm_back(grad_rot, raw, cosine, signed_sine, gain):
    grad_upper = grad_rot * cosine + half_swap(grad_rot * signed_sine)
    factor = lax.rsqrt(head_means(raw * raw) + EPSILON)
    unit_rows = raw * factor
    scaled = grad_upper * gain
    grad_lower = factor * (scaled - unit_rows * head_means(scaled * unit_rows))
    return grad_lower, jnp.sum(grad_upper * unit_rows, axis=0, keepdims=True)


def norm_rotate(raw, cosine, signed_sine, gain):
    values = raw * lax.rsqrt(head_means(raw * raw) + EPSILON) * gain
    return values * cosine + half_swap(values) * signed_sine


def attn_fwd_kernel(*refs):
    length_ref, normed, w_kv, cosine, sine, gains, tokens, gain_mid = refs[:8]
    query_hbm, out_hbm, rows_hbm, two_hbm = refs[8:12]
    q_ref, o_ref, log_ref, q_raw, k_raw, hidden, mid = refs[12:19]
    kv_hbm, three_hbm = refs[19:23], refs[23]
    w_query, w_out, kv, acc, mask, load, store, send, recv = refs[24:]
    rows, width = normed.shape
    half = KVH * HD
    dp, mine = lax.axis_index("dp"), lax.axis_index("ctx")
    middle = (mine == 1) | (mine == 2)

    loads = [
        pltpu.make_async_copy(query_hbm, w_query, load.at[0]),
        pltpu.make_async_copy(out_hbm, w_out, load.at[1]),
    ]

    def lift(k):
        return remote(kv.at[0], kv.at[k], send.at[k - 1], recv.at[k - 1], dp, mine + k)

    lift_on = remote(kv.at[2], kv.at[3], send.at[2], recv.at[2], dp, mine + 1)
    rows_three = remote(rows_hbm, three_hbm, send.at[3], recv.at[3], dp, mine ^ 3)
    rows_on = remote(two_hbm, three_hbm, send.at[4], recv.at[3], dp, mine ^ 1)

    def keep(k):
        return pltpu.make_async_copy(kv.at[k], kv_hbm[k], store.at[k])

    for copy in loads:
        copy.start()
    greet(dp, mine, (), (1, 2, 3))

    for i in range(2):
        cols = slice(4 * i * HD, (4 * i + 4) * HD)
        raw = mdot(normed[...], w_kv[:, cols])
        k_raw[:, cols] = raw
        for j in range(2):
            part = slice(2 * j * HD, (2 * j + 2) * HD)
            turned = norm_rotate(raw[:, part], cosine[...], sine[...], gains[1:2, :])
            kv[0, 0, :, (4 * i + 2 * j) * HD : (4 * i + 2 * j + 2) * HD] = turned.astype(bf16)
        value = mdot(normed[...], w_kv[:, half + 4 * i * HD : half + (4 * i + 4) * HD])
        kv[0, 1, :, cols] = value.astype(bf16)

    @pl.when(mine <= 2)
    def _():
        lift(1).start()

    @pl.when(mine <= 1)
    def _():
        lift(2).start()

    @pl.when(mine == 1)
    def _():
        rows_on.start()

    @pl.when(mine == 2)
    def _():
        rows_three.start()

    keep(0).start()
    mask[...] = causal_mask(rows, length_ref[0] - mine * rows, 1)
    loads[0].wait()

    def make_query(i, carry):
        cols = pl.ds(pl.multiple_of(i * 2 * GROUP * HD, 2 * GROUP * HD), 2 * GROUP * HD)
        raw = mdot(normed[...], w_query[:, cols])
        q_raw[:, cols] = raw
        turned = [
            norm_rotate(
                raw[:, 2 * j * HD : (2 * j + 2) * HD], cosine[...], sine[...], gains[0:1, :]
            )
            for j in range(GROUP)
        ]
        low = jnp.concatenate(turned, 1).astype(bf16)
        q_ref[:, cols] = (low.astype(f32) * (HD**-0.5)).astype(bf16)
        return carry

    lax.fori_loop(0, PAIRS, make_query, 0)

    def attend(k):
        def pairs(i, carry):
            two = pl.ds(pl.multiple_of(i * 2 * HD, 2 * HD), 2 * HD)
            cols = pl.ds(pl.multiple_of(i * 2 * GROUP * HD, 2 * GROUP * HD), 2 * GROUP * HD)
            both_keys, both_values, queries = kv[k, 0, :, two], kv[k, 1, :, two], q_ref[:, cols]
            for pair in range(2):
                keys = both_keys[:, pair * HD : (pair + 1) * HD]
                values = both_values[:, pair * HD : (pair + 1) * HD]
                extended = jnp.concatenate([values, jnp.ones_like(values)], -1)
                for g in range(GROUP):
                    h = pair * GROUP + g
                    scores = mdot(queries[:, h * HD : (h + 1) * HD], keys, NT)
                    if k == 0:
                        scores = scores + mask[...]
                    term = mdot(jnp.exp(scores).astype(bf16), extended)
                    place = 2 * GROUP * i + h
                    acc[place] = term if k == 0 else acc[place] + term
            return carry

        lax.fori_loop(0, PAIRS, pairs, 0)

    attend(0)
    for k in (1, 2, 3):

        @pl.when(mine >= k)
        def _():
            (lift_on if k == 3 else lift(k)).wait_recv()
            if k == 2:

                @pl.when(mine == 2)
                def _():
                    lift_on.start()
                    rows_on.start()

            keep(k).start()
            attend(k)

        if k == 1:

            @pl.when(mine <= 1)
            def _():
                lift(1).wait_send()
                lift(2).wait_send()

            @pl.when(mine == 1)
            def _():
                rows_three.start()

    lane = lax.broadcasted_iota(jnp.int32, (rows, 2 * HD), 1)

    def finish(i, carry):
        cols = pl.ds(pl.multiple_of(i * 2 * GROUP * HD, 2 * GROUP * HD), 2 * GROUP * HD)
        logs = jnp.zeros((rows, 2 * HD), f32)
        heads = []
        for h in range(2 * GROUP):
            full = acc[2 * GROUP * i + h]
            total = full[:, HD : HD + 1]
            heads.append(full[:, :HD] / total)
            logs = jnp.where(lane == h, jnp.log(total), logs)
        o_ref[:, cols] = jnp.concatenate(heads, 1).astype(bf16)
        log_ref[i] = jnp.transpose(logs)[:8]
        return carry

    lax.fori_loop(0, PAIRS, finish, 0)

    loads[1].wait()
    tile = 256

    def project(t, carry):
        cols = pl.ds(pl.multiple_of(t * tile, tile), tile)
        hidden[:, cols] = tokens[:, cols].astype(f32) + mdot(o_ref[...], w_out[cols, :], NT)
        return carry

    lax.fori_loop(0, width // tile, project, 0)
    value = hidden[...]
    factor = lax.rsqrt(jnp.mean(value * value, axis=-1, keepdims=True) + EPSILON)
    mid[...] = (value * factor * gain_mid[...]).astype(bf16)

    rows_three.wait_recv()

    @pl.when(middle)
    def _():
        rows_three.wait_send()
        rows_on.wait_send()

    @pl.when(mine == 2)
    def _():
        lift(1).wait_send()
        lift_on.wait_send()

    keep(0).wait()
    for k in (1, 2, 3):

        @pl.when(mine >= k)
        def _():
            keep(k).wait()


def attn_forward(length, normed, full_kv, tables, gains, tokens, gain_mid, weights, ups, cid):
    rows, width = normed.shape
    vmem = pl.BlockSpec(memory_space=pltpu.VMEM)
    keys = jax.ShapeDtypeStruct((2, rows, KVH * HD), bf16)
    rows_like = jax.ShapeDtypeStruct((rows, width), bf16)
    heads = jax.ShapeDtypeStruct((rows, H * HD), bf16)
    return pl.pallas_call(
        attn_fwd_kernel,
        in_specs=[pl.BlockSpec(memory_space=pltpu.SMEM)] + [vmem] * 7 + [ANY] * 4,
        out_specs=[vmem] * 7 + [ANY] * 5,
        out_shape=[
            heads,
            heads,
            jax.ShapeDtypeStruct((PAIRS, 8, rows), f32),
            jax.ShapeDtypeStruct((rows, H * HD), f32),
            jax.ShapeDtypeStruct((rows, KVH * HD), f32),
            jax.ShapeDtypeStruct((rows, width), f32),
            rows_like,
        ]
        + [keys] * 4
        + [rows_like],
        scratch_shapes=[
            pltpu.VMEM((width, H * HD), bf16),
            pltpu.VMEM((width, H * HD), bf16),
            pltpu.VMEM((4, 2, rows, KVH * HD), bf16),
            pltpu.VMEM((H, rows, 2 * HD), f32),
            pltpu.VMEM((rows, rows), f32),
            pltpu.SemaphoreType.DMA((2,)),
            pltpu.SemaphoreType.DMA((4,)),
            pltpu.SemaphoreType.DMA((5,)),
            pltpu.SemaphoreType.DMA((4,)),
        ],
        compiler_params=pltpu.CompilerParams(
            collective_id=cid, has_side_effects=True, vmem_limit_bytes=56 * 2**20
        ),
        name="attn_forward",
    )(length, normed, full_kv, *tables, gains, tokens, gain_mid, *weights, *ups)


def attn_bwd_kernel(blocks, length_ref, q_ref, *refs):
    kv_refs = refs[:blocks]
    do_ref, o_ref, log_ref, q_raw, k_raw, cosine, sine, gains = refs[blocks : blocks + 8]
    gq_ref, gkv_ref, gain_ref = refs[blocks + 8 : blocks + 11]
    mask, dqt, inner, own, to_send, received, send, recv = refs[blocks + 11 :]
    rows = q_ref.shape[0]
    step = pl.program_id(0)
    dp, mine = lax.axis_index("dp"), lax.axis_index("ctx")

    def give(back, i):
        return remote(
            to_send.at[back - 1, i], received.at[back - 1, i],
            send.at[back - 1, i], recv.at[back - 1, i], dp, mine - back,
        )

    @pl.when(step == 0)
    def _():
        greet(dp, mine, (), (1, 2, 3))
        mask[...] = causal_mask(rows, length_ref[0] - mine * rows, 0)
        gain_ref[...] = jnp.zeros_like(gain_ref)

    ones = jnp.ones((8, HD), bf16)
    for h in range(2 * GROUP):
        cols = slice(h * HD, (h + 1) * HD)
        product = do_ref[:, cols].astype(f32) * o_ref[:, cols].astype(f32)
        high = product.astype(bf16)
        low = (product - high.astype(f32)).astype(bf16)
        inner[h] = mdot(ones, high, NT) + mdot(ones, low, NT)

    def head(back, pair):
        cols = slice(pair * HD, (pair + 1) * HD)
        keys = kv_refs[back][0][:, cols]
        values = kv_refs[back][1][:, cols]
        keys_t = jnp.transpose(keys)
        grad_k = jnp.zeros((rows, HD), f32)
        grad_v = jnp.zeros((rows, HD), f32)
        for g in range(GROUP):
            h = pair * GROUP + g
            query = q_ref[:, h * HD : (h + 1) * HD]
            grad = do_ref[:, h * HD : (h + 1) * HD]
            scores = mdot(keys, query, NT) - log_ref[0][h : h + 1]
            if back == 0:
                scores = scores + mask[...]
            probs = jnp.exp(scores)
            gaps = mdot(values, grad, NT) - inner[h][0:1]
            grad_scores = (probs * gaps).astype(bf16)
            grad_k += mdot(grad_scores, query)
            grad_v += mdot(probs.astype(bf16), grad)
            term = mdot(keys_t, grad_scores)
            dqt[h] = term if back == 0 else dqt[h] + term
        if back == 0:
            own[step, 0, :, cols] = grad_k
            own[step, 1, :, cols] = grad_v
        else:
            to_send[back - 1, step, 0, :, cols] = grad_k.astype(bf16)
            to_send[back - 1, step, 1, :, cols] = grad_v.astype(bf16)

    def hand_over(i):
        return remote(
            to_send.at[2, i], received.at[2, i], send.at[2, i], recv.at[2, i], dp, mine - 1
        )

    def pass_on(i):
        hand_over(i).wait_recv()
        for part in range(2):
            joined = to_send[1, i, part].astype(f32) + received[2, i, part].astype(f32)
            to_send[1, i, part] = joined.astype(bf16)
        give(2, i).start()

    for pair in range(2):
        head(0, pair)
    for back in (3, 2, 1):

        @pl.when(mine >= back)
        def _():
            for pair in range(2):
                head(back, pair)
            if back == 3:
                hand_over(step).start()
            elif back == 1:
                give(1, step).start()

        if back == 2:

            @pl.when(mine == 3)
            def _():
                give(2, step).start()

    @pl.when((mine == 2) & (step > 0))
    def _():
        pass_on(step - 1)

    @pl.when((mine == 2) & (step == PAIRS - 1))
    def _():
        pass_on(step)

    for j in range(GROUP):
        cols = slice(2 * j * HD, (2 * j + 2) * HD)
        turned = jnp.concatenate([jnp.transpose(dqt[2 * j]), jnp.transpose(dqt[2 * j + 1])], 1)
        grad, gain_term = unrotate_norm_back(
            turned * (HD**-0.5), q_raw[:, cols], cosine[...], sine[...], gains[0:1, :]
        )
        gq_ref[:, cols] = grad.astype(bf16)
        gain_ref[0:1, :] += gain_term

    @pl.when(step == PAIRS - 1)
    def _():
        for back in (1, 2):

            @pl.when(mine + back < blocks)
            def _():
                for i in range(PAIRS):
                    give(back, i).wait_recv()
                    for part in range(2):
                        own[i, part] += received[back - 1, i, part].astype(f32)

        for i in range(PAIRS):
            cols = slice(2 * i * HD, (2 * i + 2) * HD)
            grad, gain_term = unrotate_norm_back(
                own[i, 0], k_raw[:, cols], cosine[...], sine[...], gains[1:2, :]
            )
            gkv_ref[:, cols] = grad.astype(bf16)
            gkv_ref[:, KVH * HD + 2 * i * HD : KVH * HD + (2 * i + 2) * HD] = own[i, 1].astype(bf16)
            gain_ref[1:2, :] += gain_term
        for back in (1, 2, 3):

            @pl.when(mine >= back)
            def _():
                for i in range(PAIRS):
                    (hand_over(i) if back == 3 else give(back, i)).wait_send()


def kv_spec(rows):
    return pl.BlockSpec((2, rows, 2 * HD), lambda i, *_: (0, 0, i))


def head_spec(rows):
    return pl.BlockSpec((rows, 2 * GROUP * HD), lambda i, *_: (0, i))


def log_spec(rows):
    return pl.BlockSpec((1, 8, rows), lambda i, *_: (i, 0, 0))


def whole_spec(*shape):
    return pl.BlockSpec(shape, lambda i, *_: (0,) * len(shape))


def attn_backward(length, query, kv_blocks, grad, mixed, logs, q_raw, k_raw, tables, gains, cid):
    rows, blocks = query.shape[0], len(kv_blocks)
    pair = (2, rows, 2 * HD)
    return pl.pallas_call(
        functools.partial(attn_bwd_kernel, blocks),
        grid=(PAIRS,),
        in_specs=[pl.BlockSpec(memory_space=pltpu.SMEM), head_spec(rows)]
        + [kv_spec(rows)] * blocks
        + [head_spec(rows), head_spec(rows), log_spec(rows), head_spec(rows)]
        + [whole_spec(rows, KVH * HD)]
        + [whole_spec(rows, 2 * HD)] * 2
        + [whole_spec(2, 2 * HD)],
        out_specs=[
            head_spec(rows),
            whole_spec(rows, 2 * KVH * HD),
            whole_spec(2, 2 * HD),
        ],
        out_shape=[
            jax.ShapeDtypeStruct((rows, H * HD), bf16),
            jax.ShapeDtypeStruct((rows, 2 * KVH * HD), bf16),
            jax.ShapeDtypeStruct((2, 2 * HD), f32),
        ],
        scratch_shapes=[
            pltpu.VMEM((rows, rows), f32),
            pltpu.VMEM((2 * GROUP, HD, rows), f32),
            pltpu.VMEM((2 * GROUP, 8, rows), f32),
            pltpu.VMEM((PAIRS,) + pair, f32),
            pltpu.VMEM((blocks - 1, PAIRS) + pair, bf16),
            pltpu.VMEM((blocks - 1, PAIRS) + pair, bf16),
            pltpu.SemaphoreType.DMA((blocks - 1, PAIRS)),
            pltpu.SemaphoreType.DMA((blocks - 1, PAIRS)),
        ],
        compiler_params=pltpu.CompilerParams(
            collective_id=cid, has_side_effects=True, vmem_limit_bytes=56 * 2**20
        ),
        cost_estimate=lasting(120),
        name="attn_backward",
    )(length, query, *kv_blocks, grad, mixed, logs, q_raw, k_raw, *tables, gains)


def feed_forward_kernel(dp_blocks, *refs):
    mid_hbm, gate_hbm, up_hbm, down_hbm = refs[:4]
    ups_hbm = refs[4:8]
    grad_ref, parts_hbm, dw_hbm = refs[8:11]
    mids, ups, w_gate, w_up, w_down, act, grad_g, grad_u, to_send, received, staged = refs[11:22]
    load, store, out_sem, send, recv = refs[22:]
    rows, width = mid_hbm.shape
    hidden = gate_hbm.shape[1]
    share = width // dp_blocks
    tile, whole = 256, hidden // 256
    dp, ctx = lax.axis_index("dp"), lax.axis_index("ctx")
    middle = (ctx == 1) | (ctx == 2)

    def slot(ref, r):
        return ref.at[pl.ds(pl.multiple_of(r * rows, rows), rows)]

    def give(r):
        return remote(mid_hbm, slot(mids, r), send.at[r], recv.at[r], dp, ctx ^ r)

    relay = remote(slot(mids, 2), slot(mids, 3), send.at[0], recv.at[3], dp, ctx ^ 1)

    def back(r):
        return remote(
            to_send.at[r - 1], received.at[r - 1], send.at[3 + r], recv.at[3 + r], dp, ctx ^ r
        )

    def load_ups(r, source):
        return pltpu.make_async_copy(source, slot(ups, r), load.at[r])

    own = pltpu.make_async_copy(mid_hbm, slot(mids, 0), load.at[4])
    weights = [
        pltpu.make_async_copy(source, target, load.at[5 + i])
        for i, (source, target) in enumerate(
            ((gate_hbm, w_gate), (up_hbm, w_up), (down_hbm, w_down))
        )
    ]

    def put_down(r):
        return pltpu.make_async_copy(
            staged.at[lax.rem(r, 2)], parts_hbm.at[ctx ^ r], store.at[lax.rem(r, 2)]
        )

    own.start()
    for copy in weights:
        copy.start()
    for r in range(4):
        load_ups(r, ups_hbm[r]).start()
    greet(dp, ctx, (), (1, 2, 3))
    give(1).start()
    give(2).start()

    @pl.when(middle)
    def _():
        give(3).start()

    own.wait()
    for copy in weights:
        copy.wait()

    def block(r, carry):
        @pl.when(r > 0)
        def _():
            give(r).wait_recv()

        @pl.when((r == 2) & middle)
        def _():
            relay.start()

        load_ups(r, mid_hbm).wait()
        here = pl.ds(pl.multiple_of(r * rows, rows), rows)

        def activate(cols):
            value, upper = mids[here, :], ups[here, :]
            gate_proj = mdot(value, w_gate[:, cols])
            up_proj = mdot(value, w_up[:, cols])
            grad_activated = mdot(upper, w_down[:, cols])
            gate_sigmoid = jax.nn.sigmoid(gate_proj)
            silu_gate = gate_proj * gate_sigmoid
            silu_slope = gate_sigmoid * (1.0 + gate_proj * (1.0 - gate_sigmoid))
            act[here, cols] = (silu_gate * up_proj).astype(bf16)
            grad_g[here, cols] = (grad_activated * up_proj * silu_slope).astype(bf16)
            grad_u[here, cols] = (grad_activated * silu_gate).astype(bf16)

        def one(t, carry):
            activate(pl.ds(pl.multiple_of(t * tile, tile), tile))
            return carry

        lax.fori_loop(0, whole, one, 0)
        if hidden % tile:
            activate(pl.ds(whole * tile, hidden % tile))

        @pl.when(r >= 2)
        def _():
            put_down(r).wait()

        def two(t, carry):
            cols = pl.ds(pl.multiple_of(t * tile, tile), tile)
            term = mdot(grad_g[here, :], w_gate[cols, :], NT)
            term += mdot(grad_u[here, :], w_up[cols, :], NT)

            @pl.when(r == 0)
            def _():
                grad_ref[:, cols] = term

            @pl.when(r > 0)
            def _():
                to_send[lax.max(r - 1, 0), :, cols] = term.astype(bf16)

            staged[lax.rem(r, 2), :, cols] = mdot(act[here, :], w_down[cols, :], NT).astype(bf16)
            return carry

        lax.fori_loop(0, width // tile, two, 0)
        put_down(r).start()

        @pl.when(r > 0)
        def _():
            back(r).start()

        return carry

    lax.fori_loop(0, 4, block, 0)

    step = 384
    for i, (left, right, place) in enumerate(
        ((mids, grad_g, w_gate), (mids, grad_u, w_up), (ups, act, w_down))
    ):

        def put(j):
            return pltpu.make_async_copy(
                place.at[pl.ds(pl.multiple_of(j * share, share), share)],
                dw_hbm.at[j, i],
                out_sem.at[i, j],
            )

        def three(t, carry):
            cols = pl.ds(pl.multiple_of(t * step, step), step)
            place[cols, :] = mdot(left[:, cols], right[...], TN).astype(bf16)
            for k in range(step // share):
                put(t * (step // share) + k).start()
            return carry

        lax.fori_loop(0, width // step, three, 0)

    for r in (1, 2, 3):
        back(r).wait_recv()
        grad_ref[...] += received[r - 1].astype(f32)
    for r in (1, 2, 3):
        back(r).wait_send()
    give(1).wait_send()
    give(2).wait_send()

    @pl.when(middle)
    def _():
        give(3).wait_send()
        relay.wait_send()

    for r in (2, 3):
        put_down(r).wait()
    for i, place in enumerate((w_gate, w_up, w_down)):
        for j in range(dp_blocks):
            pltpu.make_async_copy(
                place.at[pl.ds(j * share, share)], dw_hbm.at[j, i], out_sem.at[i, j]
            ).wait()


def feed_forward(mid, ups, full_gate, full_up, full_down_t, dp_blocks, cid):
    rows, width = mid.shape
    hidden = full_gate.shape[1]
    weight = pltpu.VMEM((width, hidden), bf16)
    kept = pltpu.VMEM((4 * rows, hidden), bf16)
    every_row = pltpu.VMEM((4 * rows, width), bf16)
    return pl.pallas_call(
        functools.partial(feed_forward_kernel, dp_blocks),
        in_specs=[ANY] * 8,
        out_specs=[pl.BlockSpec(memory_space=pltpu.VMEM), ANY, ANY],
        out_shape=[
            jax.ShapeDtypeStruct((rows, width), f32),
            jax.ShapeDtypeStruct((4, rows, width), bf16),
            jax.ShapeDtypeStruct((dp_blocks, 3, width // dp_blocks, hidden), bf16),
        ],
        scratch_shapes=[every_row, every_row, weight, weight, weight, kept, kept, kept]
        + [
            pltpu.VMEM((3, rows, width), bf16),
            pltpu.VMEM((3, rows, width), bf16),
            pltpu.VMEM((2, rows, width), bf16),
            pltpu.SemaphoreType.DMA((8,)),
            pltpu.SemaphoreType.DMA((2,)),
            pltpu.SemaphoreType.DMA((3, dp_blocks)),
            pltpu.SemaphoreType.DMA((7,)),
            pltpu.SemaphoreType.DMA((7,)),
        ],
        compiler_params=pltpu.CompilerParams(
            collective_id=cid, has_side_effects=True, vmem_limit_bytes=63 * 2**20
        ),
        name="feed_forward",
    )(mid, full_gate, full_up, full_down_t, *ups)


def shards(
    tokens,
    seq_lens,
    gain_in,
    w_query,
    w_key,
    w_value,
    w_out,
    qk_gains,
    gain_mid,
    w_gate,
    w_up,
    w_down,
    grad_out,
):
    every = ("dp", "ctx")
    rows, width = tokens.shape
    ctx = lax.axis_size("ctx")
    world = ctx * lax.axis_size("dp")
    mine = lax.axis_index("ctx")
    share = w_query.shape[0]
    qk_share = qk_gains.shape[0]
    positions = mine * rows + jnp.arange(rows, dtype=jnp.int32)
    length = seq_lens[0]
    where = jnp.stack([mine.astype(jnp.int32), length - mine * rows])
    cosine_table, sine_table = rope_tables(positions, HD)

    small = (lax.axis_size("dp"), ctx) == (8, 4)

    def move(block, pairs):
        return lax.ppermute(block, "ctx", pairs)

    def lift(block):
        one = move(block, [(0, 1), (1, 2), (2, 3)])
        two = move(block, [(0, 2), (1, 3)])
        return [block, one, two, move(block, [(0, 3)])]

    def after(value, *others):
        return lax.optimization_barrier((value, others))[0]

    def swap(block, r):
        return move(block, [(i, i ^ r) for i in range(ctx)])

    def gather(blocks, riding, hops, cid):
        if small:
            return gather_all(blocks, riding, hops, cid)
        full = [lax.all_gather(b, every, axis=0, tiled=True) for b in blocks]
        return full + [swap(b, r) for b, r in zip(riding, hops)]

    def collect(lefts, rights, norm_in, home, cid):
        if small:
            return sum_all(lefts, rights, norm_in, home, cid)
        query_weight, kv_weight, _, gain_vec, grad_above, gain_rows = norm_in
        upper = mdot(rights[1], query_weight, NT)
        upper += mdot(rights[2], kv_weight[:, : 2 * KVH * HD], NT)
        factor = rms_scale(inputs, gain_vec)[1]
        lower, gain_terms = norm_back(upper, inputs, factor, gain_vec)
        columns = jnp.concatenate([jnp.sum(gain_terms, axis=0, keepdims=True), gain_rows], 0).T
        columns = jnp.pad(columns, ((0, 0), (0, 125))).astype(bf16)
        terms = [mdot(a, b, TN).astype(bf16) for a, b in zip(lefts, rights)] + [columns]
        sums = [
            lax.psum_scatter(t, every, scatter_dimension=0, tiled=True).astype(f32) for t in terms
        ]
        far = home[mine ^ 3]
        passed = move(far, [(0, 1), (3, 2)])
        two = (home[mine ^ 2].astype(f32) + passed.astype(f32)).astype(bf16)
        landed = [swap(home[mine ^ 1], 1), swap(two, 2), move(far, [(1, 2), (2, 1)])]
        return sums + [grad_above + lower] + landed

    extra = jnp.stack([gain_in, gain_mid, jnp.pad(qk_gains, (0, share - qk_share))], 1)
    extra = jnp.pad(extra, ((0, 0), (0, 125)))
    valid_rows = (positions < length).astype(f32)[:, None]
    upstream = grad_out.astype(f32) * valid_rows
    upstream_low = upstream.astype(bf16)
    full_kv, full_query, full_out_t, ups_near, ups_two = gather(
        [jnp.concatenate([w_key, w_value, extra], 1), w_query, w_out.T],
        [upstream_low, upstream_low],
        (1, 2),
        1,
    )
    kv_width = 2 * KVH * HD
    full_extra = full_kv[:, kv_width:].astype(f32)
    full_gain_in, full_gain_mid = full_extra[:, 0], full_extra[:, 1]
    full_qk = full_extra[:, 2].reshape(world, share)[:, :qk_share].reshape(-1)
    full_gate = lax.all_gather(w_gate, "dp", axis=0, tiled=True)
    full_up = lax.all_gather(after(w_up, full_kv, full_gate), "dp", axis=0, tiled=True)
    full_down_t = lax.all_gather(after(w_down.T, full_kv, full_gate), "dp", axis=0, tiled=True)
    wide_kv, full_kv = full_kv, full_kv[:, :kv_width]

    inputs = tokens.astype(f32)

    normed_f, factor_in = rms_scale(inputs, full_gain_in)
    normed = normed_f.astype(bf16)
    flat_cosine = jnp.concatenate([cosine_table[:, 0], cosine_table[:, 0]], 1)
    flat_sine = jnp.concatenate([sine_table[:, 0], sine_table[:, 0]], 1)
    turn_sign = jnp.where(jnp.arange(2 * HD) % HD < HD // 2, -1.0, 1.0).astype(f32)
    tables = (flat_cosine, flat_sine * turn_sign)
    pair_gains = jnp.concatenate([full_qk.reshape(2, HD), full_qk.reshape(2, HD)], 1)
    query_low, mixed_low, logs, query_flat, key_flat, hidden, normed_mid, *landed = attn_forward(
        seq_lens,
        normed,
        wide_kv,
        tables,
        pair_gains,
        tokens,
        full_gain_mid[None],
        (full_query, full_out_t),
        (upstream_low, ups_two),
        3,
    )
    kv_blocks = landed[:4]
    ups = [upstream_low, ups_near, ups_two] + landed[4:]
    factor_mid = rms_scale(hidden, full_gain_mid)[1]

    grad_mid_term, down_parts, grad_ffn = feed_forward(
        normed_mid, ups, full_gate, full_up, full_down_t, lax.axis_size("dp"), 2
    )
    grad_ffn = lax.psum_scatter(
        grad_ffn.reshape(-1, grad_ffn.shape[-1]), "dp", scatter_dimension=0, tiled=True
    )
    grad_hidden_norm, gain_terms_mid = norm_back(grad_mid_term, hidden, factor_mid, full_gain_mid)
    grad_hidden = upstream + grad_hidden_norm
    grad_branch = grad_hidden.astype(bf16)
    grad_mixed = mdot(grad_branch, full_out_t).astype(bf16)

    grad_query_low, grad_kv_low, gain_rows = attn_backward(
        seq_lens,
        query_low,
        kv_blocks,
        grad_mixed,
        mixed_low,
        logs,
        query_flat,
        key_flat,
        tables,
        pair_gains,
        5,
    )
    grad_qk = (gain_rows[:, :HD] + gain_rows[:, HD:]).reshape(-1)
    qk_row = jnp.pad(grad_qk.reshape(world, qk_share), ((0, 0), (0, share - qk_share)))
    other_gains = jnp.stack([jnp.sum(gain_terms_mid, axis=0), qk_row.reshape(-1)])
    grad_wout, sum_query, sum_kv, sum_extra, grad_tokens, *down_terms = collect(
        (grad_branch, normed, normed),
        (mixed_low, grad_query_low, grad_kv_low),
        (full_query, wide_kv, tokens, full_gain_in[None], grad_hidden, other_gains),
        down_parts,
        4,
    )
    inner = (mine == 1) | (mine == 2)
    down_terms = [down_parts[mine], *down_terms[:2], jnp.where(inner, down_terms[2], 0)]
    grad_ffn, down_terms = after((grad_ffn, down_terms), sum_kv)
    output = (hidden + sum(t.astype(f32) for t in down_terms)).astype(bf16)
    grad_wgate, grad_wup, grad_wdown = (
        grad_ffn[i * w_gate.shape[0] : (i + 1) * w_gate.shape[0]].astype(f32) for i in range(3)
    )
    grad_wdown = grad_wdown.T
    return (
        output,
        grad_tokens,
        sum_extra[:, 0],
        sum_query,
        sum_kv[:, : KVH * HD],
        sum_kv[:, KVH * HD :],
        grad_wout.T,
        sum_extra[:qk_share, 2],
        sum_extra[:, 1],
        grad_wgate,
        grad_wup,
        grad_wdown,
    )


def solution(mesh):
    every = ("dp", "ctx")
    rows, one = P(every, None), P(every)
    in_specs = (
        rows,
        P("dp"),
        one,
        rows,
        rows,
        rows,
        P(None, every),
        one,
        one,
        P("dp", "ctx"),
        P("dp", "ctx"),
        P("ctx", "dp"),
        rows,
    )
    out_specs = (
        rows,
        rows,
        one,
        rows,
        rows,
        rows,
        P(None, every),
        one,
        one,
        P("dp", "ctx"),
        P("dp", "ctx"),
        P("ctx", "dp"),
    )
    return jax.shard_map(shards, mesh=mesh, in_specs=in_specs, out_specs=out_specs, check_vma=False)
```
